128 devices in a mesh: seq: 8 (over x, core), dp: 16 (over z, y).
Axes of the slice: x: 4, y: 4, z: 4, core: 2. Of those that a mesh axis runs over, the one named last changes fastest.
Arguments:
- tokens: bfloat16 [4, 16, 64, 128, 256], P(None, 'dp', 'seq'), may hold values from -6 to 6
- lengths: int32 [4, 16, 64], P(None, 'dp'), may hold values from 1 to 64, as said below
- visible: int32 [4, 16, 64, 128], P(None, 'dp'), may hold values from 0 to 1, as said below
- norm_gains: bfloat16 [2, 256], P(None, ('seq', 'dp')), may hold values from 0.5 to 1.5
- norm_biases: bfloat16 [2, 256], P(None, ('seq', 'dp')), may hold values from -1.25 to 1.25
- w_qkv: bfloat16 [256, 768], P(('seq', 'dp')), may hold values from -0.5 to 0.5
- w_out: bfloat16 [256, 256], P(('seq', 'dp')), may hold values from -1.5 to 1.5
- w_up: bfloat16 [256, 1024], P(('seq', 'dp')), may hold values from -0.375 to 0.375
- w_down: bfloat16 [1024, 256], P(('seq', 'dp')), may hold values from -0.1875 to 0.1875
- proj_biases: bfloat16 [4, 256], P(None, ('seq', 'dp')), may hold values from -1.25 to 1.25
- up_bias: bfloat16 [1024], P(('seq', 'dp')), may hold values from -1.25 to 1.25
- mask_token: bfloat16 [256], P(('seq', 'dp')), may hold values from -6 to 6
- time_embed: bfloat16 [64, 256], P(None, ('seq', 'dp')), may hold values from -3 to 3
- dec_grad: bfloat16 [4, 16, 64, 128, 256], P(None, 'dp', None, 'seq'), may hold values from -6 to 6
Outputs:
- decoded: bfloat16 [4, 16, 64, 128, 256], P(None, 'dp', None, 'seq')
- grad_tokens: float32 [4, 16, 64, 128, 256], P(None, 'dp', 'seq')
- grad_norm_gains: float32 [2, 256], P(None, ('seq', 'dp'))
- grad_norm_biases: float32 [2, 256], P(None, ('seq', 'dp'))
- grad_w_qkv: float32 [256, 768], P(('seq', 'dp'))
- grad_w_out: float32 [256, 256], P(('seq', 'dp'))
- grad_w_up: float32 [256, 1024], P(('seq', 'dp'))
- grad_w_down: float32 [1024, 256], P(('seq', 'dp'))
- grad_proj_biases: float32 [4, 256], P(None, ('seq', 'dp'))
- grad_up_bias: float32 [1024], P(('seq', 'dp'))
- grad_mask_token: float32 [256], P(('seq', 'dp'))
- grad_time_embed: float32 [64, 256], P(None, ('seq', 'dp'))
The draws below stay inside these ranges and needn't reach their ends.
Inputs may be any that keep to these rules, and one draw needn't show every extreme that they name: `lengths`: in every micro-batch and batch one trajectory has all 64 timesteps. `visible`: slot 0 of every trajectory is 1.
All inputs are finite; a program needn't handle non-finite values.
Results may differ from the reference program's by a relative error of at most 0.015.
Values may be sent and summed in bfloat16 or wider, within the bound.
A program may use at most 192 MiB of HBM per device.

```python
import jax
import jax.numpy as jnp
from jax import lax

D = 256
HEADS = 4
FF = 1024
STEPS = 64
SLOTS = 128
TRAJ = 64
MICRO = 4
BATCHES = 16


def draw_lengths(key, part):
    key = jax.random.fold_in(key, 11)
    first_key, second_key, third_key = jax.random.split(key, 3)
    first_draw = jax.random.randint(first_key, (MICRO, BATCHES, TRAJ), 0, STEPS)
    second_draw = jax.random.randint(second_key, (MICRO, BATCHES, TRAJ), 0, STEPS)
    longest = jax.random.randint(third_key, (MICRO, BATCHES, 1), 0, TRAJ)
    shorter = 1 + first_draw * second_draw // STEPS
    traj_index = jnp.arange(TRAJ, dtype=jnp.int32)
    return jnp.where(traj_index == longest, STEPS, shorter).astype(jnp.int32)


def draw_visible(key, part):
    key = jax.random.fold_in(key, 23)
    coin_flips = jax.random.randint(key, (MICRO, BATCHES, TRAJ, SLOTS), 0, 2)
    slot_index = jnp.arange(SLOTS, dtype=jnp.int32)
    return jnp.where(slot_index == 0, 1, coin_flips).astype(jnp.int32)


def block_scale(own_key, extent, shards, low, high):
    def one(dim, blocks):
        steps = jax.random.uniform(jax.random.fold_in(jax.random.fold_in(own_key, 6), dim), (blocks,), jnp.float32, low / len(shards), high / len(shards))
        return jnp.repeat(jnp.exp(steps), extent[dim] // blocks).reshape((-1,) + (1,) * (len(extent) - dim - 1))

    level = one(*shards[0])
    for cut in shards[1:]:
        level = level * one(*cut)
    return level


def noise(rng, shape, deviation, bound, pieces=(), kind=jnp.bfloat16):
    drawn = deviation * jax.random.normal(rng, shape, jnp.float32)
    if pieces:
        drawn = drawn * block_scale(rng, shape, pieces, -0.22, 0.18)
    return jnp.clip(drawn, -bound, bound).astype(kind)


def setup_inputs(seed: int = 0) -> dict:
    key_list = jax.random.split(jax.random.key(seed), 15)
    return {
        "tokens": noise(key_list[0], (MICRO, BATCHES, TRAJ, SLOTS, D), 1.0, 6.0, ((1, 16), (2, 8))),
        "lengths": draw_lengths(jax.random.fold_in(key_list[14], 71), 0),
        "visible": draw_visible(jax.random.fold_in(key_list[14], 71), 0),
        "norm_gains": jnp.clip(1.0 + 0.1 * jax.random.normal(key_list[3], (2, D), jnp.float32), 0.5, 1.5).astype(jnp.bfloat16),
        "norm_biases": noise(key_list[4], (2, D), 0.2, 1.25, ((1, 128),)),
        "w_qkv": noise(key_list[5], (D, 3 * D), (D // 2) ** -0.5, 0.5, ((0, 128),)),
        "w_out": noise(key_list[6], (D, D), (D // 16) ** -0.5, 1.5, ((0, 128),)),
        "w_up": noise(key_list[7], (D, FF), D ** -0.5, 0.375, ((0, 128),)),
        "w_down": noise(key_list[8], (FF, D), FF ** -0.5, 0.1875, ((0, 128),)),
        "proj_biases": noise(key_list[9], (4, D), 0.2, 1.25, ((1, 128),)),
        "up_bias": noise(key_list[10], (FF,), 0.2, 1.25, ((0, 128),)),
        "mask_token": noise(key_list[11], (D,), 1.0, 6.0, ((0, 128),)),
        "time_embed": noise(key_list[12], (STEPS, D), 0.5, 3.0, ((1, 128),)),
        "dec_grad": noise(key_list[13], (MICRO, BATCHES, TRAJ, SLOTS, D), 1.0, 6.0, ((1, 16), (3, 8))),
    }


@jax.custom_vjp
def low(v):
    return lax.optimization_barrier(v.astype(jnp.bfloat16)).astype(jnp.float32)

@jax.custom_vjp
def low_back(v):
    return v

def low_keep(v):
    return (low(v), None)

def low_pass(kept, grad):
    return (grad,)

def back_keep(v):
    return (v, None)

def back_low(kept, grad):
    return (low(grad),)
low.defvjp(low_keep, low_pass)
low_back.defvjp(back_keep, back_low)
NORM_EPS = 1e-05
HIGHEST = lax.Precision.HIGHEST

def layer_norm(values_in, gain_row, shift_row):
    centre = values_in - lax.optimization_barrier(jnp.mean(values_in, axis=-1, keepdims=True))
    spread = lax.optimization_barrier(jnp.mean(centre * centre, axis=-1, keepdims=True))
    return centre * lax.rsqrt(spread + NORM_EPS) * gain_row + shift_row

def project(left_side, right_side):
    return jnp.einsum('tpi,ij->tpj', left_side, right_side, precision=HIGHEST)

def block_forward(params, inputs):
    norm_gains, norm_biases, w_qkv, w_out, w_up, w_down, proj_biases, up_bias, mask_token, time_embed = params
    block_tokens, key_open, valid_rows, shown_rows = inputs
    model_width = block_tokens.shape[-1]
    head_size = model_width // HEADS
    traj_count = block_tokens.shape[0]
    slot_count = block_tokens.shape[1]
    head_shape = (traj_count, slot_count, HEADS, head_size)
    normed_first = low(layer_norm(block_tokens, norm_gains[0], norm_biases[0]))
    qkv_bias = jnp.concatenate([proj_biases[0], jnp.zeros_like(proj_biases[0]), proj_biases[1]])
    qkv_rows = low(low_back(project(normed_first, w_qkv) + qkv_bias))
    queries = qkv_rows[..., :model_width].reshape(head_shape)
    keys_all = qkv_rows[..., model_width:2 * model_width].reshape(head_shape)
    values_all = qkv_rows[..., 2 * model_width:].reshape(head_shape)
    scores = jnp.einsum('tqhd,tkhd->thqk', queries, keys_all, precision=HIGHEST) * head_size ** (-0.5)
    scores = low_back(jnp.where(key_open[:, None, None, :] > 0, scores, -1e+30))
    shifted = jnp.exp(scores - lax.optimization_barrier(jnp.max(scores, axis=-1, keepdims=True)))
    weights = shifted / lax.optimization_barrier(jnp.sum(shifted, axis=-1, keepdims=True))
    attended = jnp.einsum('thqk,tkhd->tqhd', low(weights), values_all, precision=HIGHEST)
    attended = low(low_back(attended.reshape(traj_count, slot_count, model_width)))
    mixed_rows = block_tokens + low_back(project(attended, w_out) + proj_biases[2])
    normed_second = low(layer_norm(mixed_rows, norm_gains[1], norm_biases[1]))
    hidden_pre = low_back(project(normed_second, w_up) + up_bias)
    hidden_act = low(jax.nn.gelu(hidden_pre, approximate=True))
    encoded = mixed_rows + low_back(project(hidden_act, w_down) + proj_biases[3])
    step_rows = jnp.repeat(time_embed, 2, axis=0)
    chosen = jnp.where(shown_rows[..., None] > 0, low(encoded), mask_token)
    return valid_rows[..., None] * (chosen + step_rows)

def reference(tokens, lengths, visible, norm_gains, norm_biases, w_qkv, w_out, w_up, w_down, proj_biases, up_bias, mask_token, time_embed, dec_grad):
    params = tuple((argument.astype(jnp.float32) for argument in (norm_gains, norm_biases, w_qkv, w_out, w_up, w_down, proj_biases, up_bias, mask_token, time_embed)))
    flat_shape = (MICRO * BATCHES, TRAJ, SLOTS, D)
    mask_shape = (MICRO * BATCHES, TRAJ, SLOTS)
    token_blocks = tokens.astype(jnp.float32).reshape(flat_shape)
    slot_index = jnp.arange(SLOTS, dtype=jnp.int32)
    valid_rows = (slot_index // 2 < lengths[..., None]).astype(jnp.float32).reshape(mask_shape)
    shown_rows = (visible > 0).astype(jnp.float32).reshape(mask_shape)
    key_open = valid_rows * shown_rows

    def whole_layer(token_input, layer_params):

        def one_block(inputs):
            return block_forward(layer_params, inputs)
        return lax.map(jax.checkpoint(one_block), (token_input, key_open, valid_rows, shown_rows))
    decoded, pullback = jax.vjp(whole_layer, token_blocks, params)
    token_grad, param_grads = pullback(dec_grad.astype(jnp.float32).reshape(flat_shape))
    return (decoded.astype(jnp.bfloat16).reshape(tokens.shape), token_grad.reshape(tokens.shape), param_grads[0], param_grads[1], param_grads[2], param_grads[3], param_grads[4], param_grads[5], param_grads[6], param_grads[7], param_grads[8], param_grads[9])
```

```python
import functools

import jax
import jax.numpy as jnp
from jax import lax
from jax.experimental import pallas as pl
from jax.experimental.pallas import tpu as pltpu
from jax.sharding import PartitionSpec as P

f32, bf16, i32 = jnp.float32, jnp.bfloat16, jnp.int32
EPS = 1e-5
BIG = 1e30
D, FF, SL, MICRO, TRAJ = 256, 1024, 128, 4, 64
NT = 32
PART = 512
GELU_A = 0.7978845608028654
GELU_B = 0.044715
CAPS = (304, 240, 192, 160, 128, 80, 64, 48)
FULL = (PART,) * 8
MESH = pl.DeviceIdType.MESH
VMEM_LIMIT = 56 * 2**20

TE, GAIN, SHIFT, BIAS, MASK, UP, FLAG = 0, 64, 66, 68, 72, 80, 96


def nt_dot(a, b):
    return lax.dot_general(a, b, (((1,), (1,)), ((), ())), preferred_element_type=f32)


def nn_dot(a, b):
    return lax.dot_general(a, b, (((1,), (0,)), ((), ())), preferred_element_type=f32)


def tn_dot(a, b):
    return lax.dot_general(a, b, (((0,), (0,)), ((), ())), preferred_element_type=f32)


def iota(shape, dim):
    return lax.broadcasted_iota(i32, shape, dim)


def one_zero(cond):
    return jnp.where(cond, 1.0, 0.0)


def fold8(v):
    n = v.shape[0] // 8
    return jnp.sum(v.reshape(n, 8, v.shape[1]), axis=0)


def bases(caps):
    out, at = [], 0
    for c in caps:
        out.append(at)
        at += c
    return out


def decode_room(caps):
    most = max(caps)
    return most, -(-(most + 16) // SL) * SL


class Place:
    def __init__(self):
        self.seq = lax.axis_index("seq")
        self.dp = lax.axis_index("dp")
        self.x, self.core = self.seq // 2, self.seq % 2
        self.z, self.y = self.dp // 4, self.dp % 4

    def seq_peer(self, k):
        return ((self.seq + k) % 8, self.dp)

    def x_peer(self, k):
        return ((self.seq + 2 * k) % 8, self.dp)

    def y_peer(self, k):
        return (self.seq, self.z * 4 + (self.y + k) % 4)

    def z_peer(self, k):
        return (self.seq, ((self.z + k) % 4) * 4 + self.y)

    def sibling(self):
        return (self.seq + 1 - 2 * self.core, self.dp)

    def greet(self, everyone=True):
        peers = [self.seq_peer(k) for k in range(1, 8)]
        if everyone:
            peers += [self.y_peer(k) for k in range(1, 4)] + [self.z_peer(k) for k in range(1, 4)]
        barrier = pltpu.get_barrier_semaphore()
        for peer in peers:
            pl.semaphore_signal(barrier, inc=1, device_id=peer, device_id_type=MESH)
        return barrier, len(peers)


def remote(src, dst, send_sem, recv_sem, peer):
    return pltpu.make_async_remote_copy(
        src_ref=src, dst_ref=dst, send_sem=send_sem, recv_sem=recv_sem, device_id=peer, device_id_type=MESH
    )


def mask_rows(len_ref, vis_ref):
    eye = one_zero(iota((TRAJ, TRAJ), 0) == iota((TRAJ, TRAJ), 1)).astype(bf16)
    step = (iota((TRAJ, SL), 1) // 2).astype(f32)
    valid, shown = [], []
    for m in range(MICRO):
        row = jnp.broadcast_to(len_ref[m : m + 1, :].astype(f32), (SL, TRAJ)).astype(bf16)
        valid.append(one_zero(step < nt_dot(eye, row)))
        shown.append(one_zero(vis_ref[m] > 0))
    return jnp.concatenate(valid, axis=0), jnp.concatenate(shown, axis=0)


def part_lanes(valid, shown, part):
    n = MICRO * TRAJ
    pick = one_zero(iota((SL, PART), 0) == 16 * part + iota((SL, PART), 1) % 16).astype(bf16)
    row, lane = iota((n, PART), 0), iota((n, PART), 1)
    mine = (row // TRAJ == lane // SL) & (row % 8 == (lane % SL) // 16)
    group = one_zero((iota((16, n), 1) % TRAJ) // 8 == iota((16, n), 0)).astype(bf16)

    def lanes(mask):
        spread = nn_dot(mask.astype(bf16), pick)
        return nn_dot(group, jnp.where(mine, spread, 0.0).astype(bf16))[:8]

    return lanes(valid), lanes(shown)


def part_ranks(open_lanes):
    r, c = iota((PART, PART), 0), iota((PART, PART), 1)
    tri = (one_zero(r < c) - jnp.where(r == c, 512.0, 0.0)).astype(bf16)
    rows = jnp.concatenate([open_lanes, jnp.zeros((8, PART), f32)], axis=0).astype(bf16)
    return nn_dot(rows, tri)[:8]


def pack_part(caps, owner, rank_ref, ext_ref, dg_ref):
    most = max(caps)
    row = iota((most, PART), 0).astype(f32)
    hit = one_zero(rank_ref[pl.ds(owner, 1), :] + 512.0 == row)
    lhs = jnp.concatenate([hit, ext_ref[owner]], axis=0).astype(bf16)
    first = pl.multiple_of(owner * 8, 8)
    parts = [dg_ref[m, pl.ds(first, 8)].reshape(SL, D) for m in range(MICRO)]
    return nn_dot(lhs, jnp.concatenate(parts, axis=0))


def prepare_part(me, len_ref, vis_ref, rank_scr, ext_scr):
    valid, shown = mask_rows(len_ref, vis_ref)
    v8, s8 = part_lanes(valid, shown, me.seq)
    rank_scr[...] = part_ranks(v8 * s8)
    lane_step = (iota((8, PART), 1) % 16) // 2
    step_row = iota((8, PART), 0)
    for i in range(8):
        v = v8[i : i + 1, :]
        steps = jnp.where(lane_step == step_row, jnp.broadcast_to(v, (8, PART)), 0.0)
        hidden = jnp.where(step_row == 0, jnp.broadcast_to(v * (1.0 - s8[i : i + 1, :]), (8, PART)), 0.0)
        ext_scr[i] = jnp.concatenate([steps, hidden], axis=0)
    return valid, shown


def send_part(caps, me, k, dg_ref, rank_scr, ext_scr, buf, r_ref, sends, recvs):
    most = max(caps)
    base = bases(caps)
    owner = (me.seq + k) % 8
    got = pack_part(caps, owner, rank_scr, ext_scr, dg_ref)
    buf[k] = got[:most].astype(bf16)
    for j in range(8):
        @pl.when(me.seq == j)
        def _():
            there = r_ref.at[pl.ds(base[j], caps[j])]
            if k == 0:
                there[...] = buf[k, : caps[j]]
            else:
                remote(buf.at[k, pl.ds(0, caps[j])], there, sends.at[k], recvs.at[j], me.seq_peer(k)).start()
    return got[most:]


def finish_parts(caps, me, buf, r_ref, sends, recvs):
    base = bases(caps)
    for j in range(8):
        @pl.when(me.seq != j)
        def _():
            here = r_ref.at[pl.ds(base[j], caps[j])]
            pltpu.make_async_copy(here, here, recvs.at[j]).wait()

        @pl.when(me.seq == j)
        def _():
            for k in range(1, 8):
                there = buf.at[k, pl.ds(0, caps[j])]
                pltpu.make_async_copy(there, there, sends.at[k]).wait()


def exchange_kernel(caps, len_ref, vis_ref, dg_ref, r_ref, rank_scr, ext_scr, buf, sends, recvs):
    me = Place()
    barrier, count = me.greet(everyone=False)
    prepare_part(me, len_ref, vis_ref, rank_scr, ext_scr)
    pl.semaphore_wait(barrier, count)
    for k in range(8):
        send_part(caps, me, k, dg_ref, rank_scr, ext_scr, buf, r_ref, sends, recvs)
    finish_parts(caps, me, buf, r_ref, sends, recvs)


def vmem():
    return pl.BlockSpec(memory_space=pltpu.VMEM)


def part_scratch(caps):
    return [
        pltpu.VMEM((8, PART), f32),
        pltpu.VMEM((8, 16, PART), f32),
        pltpu.VMEM((8, max(caps), D), bf16),
        pltpu.SemaphoreType.DMA((8,)),
        pltpu.SemaphoreType.DMA((8,)),
    ]


def exchange(caps, lengths, visible, dec_grad, cid):
    return pl.pallas_call(
        functools.partial(exchange_kernel, caps),
        out_shape=jax.ShapeDtypeStruct((sum(caps), D), bf16),
        in_specs=[vmem()] * 3,
        out_specs=vmem(),
        scratch_shapes=part_scratch(caps),
        compiler_params=pltpu.CompilerParams(collective_id=cid, has_side_effects=True, vmem_limit_bytes=VMEM_LIMIT),
        name="exchange_gradients",
    )(lengths, visible, dec_grad)


def gather_kernel(
    caps, len_ref, vis_ref, dg_ref, wq_ref, wo_ref, wu_ref, wd_ref, small_ref,
    w_out, wdn_out, sm_out, r_ref, open_out, count_out, part_out,
    rank_scr, ext_scr, buf, sends, recvs, slabs, open_scr, s1, r1, s2a, r2a, s2b, r2b, s3, r3,
):
    me = Place()
    barrier, count = me.greet()
    half, x2 = me.x // 2, me.x % 2
    own = (me.z + half * (me.y - me.z), me.y + half * (me.z - me.y))

    valid, shown = mask_rows(len_ref, vis_ref)
    opened = valid * shown
    open_scr[...] = opened
    n = MICRO * TRAJ
    group = one_zero((iota((16, n), 1) % TRAJ) // 8 == iota((16, n), 0)).astype(bf16)
    blk = one_zero(iota((SL, SL), 0) // 16 == iota((SL, SL), 1) // 16).astype(bf16)
    pairs = nn_dot(nn_dot(group, opened.astype(bf16)).astype(bf16), blk)
    lane_blk = iota((16, SL), 1) // 16
    room = jnp.zeros((16, SL), f32)
    for j in range(8):
        room = jnp.where(lane_blk == j, float(caps[j]), room)
    over = jnp.max(jnp.max(one_zero(pairs > room), axis=1, keepdims=True), axis=0, keepdims=True)

    small = small_ref[...].astype(f32)
    small = jnp.where(iota((2, SL), 1) == FLAG, jnp.broadcast_to(over, (2, SL)), small)
    small = jnp.concatenate([small, jnp.zeros((2, SL), f32)], axis=1)
    rows = []
    for f in range(2):
        one = slice(f, f + 1)
        rows += [wq_ref[one, c : c + D].astype(f32) for c in range(0, 3 * D, D)]
        rows += [wo_ref[one, :].astype(f32)]
        rows += [wu_ref[one, c : c + D].astype(f32) for c in range(0, 4 * D, D)]
        rows += [small[one]]
    slab = jnp.concatenate(rows + [wd_ref[...].astype(f32), jnp.zeros((6, D), f32)], axis=0)
    mine = slabs.at[half, me.core, own[0], own[1], x2]
    mine[...] = slab.astype(bf16)

    pl.semaphore_wait(barrier, count)
    step1 = [remote(mine, mine, s1.at[k], r1.at[k], me.x_peer(k + 1)) for k in range(3)]
    for c in step1:
        c.start()

    v8, s8 = part_lanes(valid, shown, me.seq)
    rank_scr[...] = part_ranks(v8 * s8)
    lane_step = (iota((8, PART), 1) % 16) // 2
    step_row = iota((8, PART), 0)
    for i in range(8):
        v = v8[i : i + 1, :]
        steps = jnp.where(lane_step == step_row, jnp.broadcast_to(v, (8, PART)), 0.0)
        hidden = jnp.where(step_row == 0, jnp.broadcast_to(v * (1.0 - s8[i : i + 1, :]), (8, PART)), 0.0)
        ext_scr[i] = jnp.concatenate([steps, hidden], axis=0)

    def send(k):
        return send_part(caps, me, k, dg_ref, rank_scr, ext_scr, buf, r_ref, sends, recvs)

    sums = jnp.zeros((16, D), f32)
    for k in (4, 3, 5, 2):
        sums = sums + send(k)
    for c in step1:
        c.wait()
    step2a = []
    row_a = slabs.at[0, me.core, me.z, me.y]
    row_b = slabs.at[1, me.core, me.y, me.z]
    for k in range(3):
        step2a.append(remote(row_a, row_a, s2a.at[0, k], r2a.at[0, k], me.y_peer(k + 1)))
        step2a.append(remote(row_b, row_b, s2a.at[1, k], r2a.at[1, k], me.z_peer(k + 1)))
    for c in step2a:
        c.start()
    for k in (6, 1, 7, 0):
        sums = sums + send(k)
    for c in step2a:
        c.wait()
    all_a = slabs.at[0, me.core, me.z]
    all_b = slabs.at[1, me.core, me.y]
    step2b, step3 = [], []
    for k in range(3):
        step2b.append(remote(all_a, all_a, s2b.at[0, k], r2b.at[0, k], me.z_peer(k + 1)))
        step2b.append(remote(all_b, all_b, s2b.at[1, k], r2b.at[1, k], me.y_peer(k + 1)))
    for c in step2b:
        c.start()
    step3.append(remote(all_a, all_a, s3.at[0, 0], r3.at[0, 0], me.sibling()))
    step3.append(remote(all_b, all_b, s3.at[1, 0], r3.at[1, 0], me.sibling()))
    for c in step3:
        c.start()

    for m in range(MICRO):
        open_out[8 * m : 8 * m + 8, :] = open_scr[pl.ds(pl.multiple_of(m * TRAJ + 8 * me.seq, 8), 8), :]
    counted = jnp.concatenate([open_out[...], jnp.zeros((SL - NT, SL), f32)], axis=0).astype(bf16)
    count_out[...] = nt_dot(jnp.ones((16, SL), bf16), counted)[:8].astype(i32)
    part_out[...] = jnp.zeros_like(part_out)
    part_out[pl.ds(pl.multiple_of(8 * me.seq, 8), 8), :] = sums[:8]
    part_out[MASK : MASK + 1, :] = sums[8:9]

    for k in range(3):
        for h in range(2):
            step2b[2 * k + h].wait()
            from_row = ((me.z if h == 0 else me.y) + 3 - k) % 4
            part = slabs.at[h, me.core, from_row]
            c = remote(part, part, s3.at[h, k + 1], r3.at[h, k + 1], me.sibling())
            c.start()
            step3.append(c)
    for c in step3:
        c.wait()

    pr, pc = iota((D, D), 0), iota((D, D), 1)
    want = jnp.where(
        pr < 144,
        ((pr % 16) // 2) * 32 + (pr % 2) * 9 + pr // 16,
        jnp.where(pr < 208, ((pr - 144) // 8) * 32 + 18 + (pr - 144) % 8, -1),
    )
    perm = one_zero(want == pc).astype(bf16)
    feature_rows = []
    for q in range(16):
        seq, z0 = q // 2, (q % 2) * 2
        x, core = seq // 2, seq % 2
        chunk = []
        for z in (z0, z0 + 1):
            for y in range(4):
                a, b = (z, y) if x < 2 else (y, z)
                chunk.append(slabs[x // 2, core, a, b, x % 2])
        got = nn_dot(perm, jnp.concatenate(chunk, axis=0)).astype(bf16)
        for b in range(8):
            w_out[16 * q : 16 * q + 16, b * D : (b + 1) * D] = got[16 * b : 16 * b + 16]
        feature_rows.append(got[128:144, :SL])
        wdn_out[64 * q : 64 * q + 64, :] = got[144:208]
    features = jnp.concatenate(feature_rows, axis=0)
    eye = one_zero(iota((SL, SL), 0) == iota((SL, SL), 1)).astype(bf16)
    sm_out[...] = nt_dot(eye, features)
    even = one_zero(iota((SL, D), 1) == 2 * iota((SL, D), 0)).astype(bf16)
    by_device = nn_dot(even, features).astype(bf16)
    spread = one_zero(iota((SL, FF), 0) == UP + iota((SL, FF), 1) % 8).astype(bf16)
    wide = jnp.where(iota((SL, FF), 0) == iota((SL, FF), 1) // 8, nn_dot(by_device, spread), 0.0).astype(bf16)
    up = nn_dot(jnp.ones((16, SL), bf16), wide)[:1]
    for c in range(4):
        sm_out[UP + c : UP + c + 1, :] = up[:, c * D : (c + 1) * D]

    finish_parts(caps, me, buf, r_ref, sends, recvs)


def gather(caps, lengths, visible, dec_grad, w_qkv, w_out, w_up, w_down, small, cid):
    dma = pltpu.SemaphoreType.DMA
    return pl.pallas_call(
        functools.partial(gather_kernel, caps),
        out_shape=(
            jax.ShapeDtypeStruct((D, 8 * D), bf16),
            jax.ShapeDtypeStruct((FF, D), bf16),
            jax.ShapeDtypeStruct((SL, D), f32),
            jax.ShapeDtypeStruct((sum(caps), D), bf16),
            jax.ShapeDtypeStruct((NT, SL), f32),
            jax.ShapeDtypeStruct((8, SL), i32),
            jax.ShapeDtypeStruct((SL, D), f32),
        ),
        in_specs=[vmem()] * 8,
        out_specs=(vmem(),) * 7,
        scratch_shapes=part_scratch(caps) + [
            pltpu.VMEM((2, 2, 4, 4, 2, 32, D), bf16),
            pltpu.VMEM((MICRO * TRAJ, SL), f32),
            dma((3,)), dma((3,)), dma((2, 3)), dma((2, 3)), dma((2, 3)), dma((2, 3)), dma((2, 4)), dma((2, 4)),
        ],
        compiler_params=pltpu.CompilerParams(collective_id=cid, has_side_effects=True, vmem_limit_bytes=VMEM_LIMIT),
        name="gather_and_exchange",
    )(lengths, visible, dec_grad, w_qkv, w_out, w_up, w_down, small)


def encoder_kernel(caps, nt_ref, o_ref, tok_ref, w_ref, wd_ref, sm_ref, r_ref, gpart_ref,
              gtok_ref, s_ref, gs_ref,
              x_scr, src_scr, srct_scr, g_scr, gw_scr, gwd_scr, sums_scr, bup_scr, pp_scr, qkv_scr, gqkv_scr, hilo_scr,
              bin_smem, start_smem):
    rtot = sum(caps)
    lane1 = iota((1, SL), 1)
    stv = jnp.zeros((1, SL), f32)
    env = jnp.zeros((1, SL), f32)
    bnv = jnp.full((1, SL), -1.0, f32)
    b = jnp.int32(0)
    off = jnp.int32(0)
    for t in range(NT):
        n = nt_ref[0, t]
        over = (off + n) > SL
        b = jnp.where(over, b + 1, b)
        off = jnp.where(over, 0, off)
        bin_smem[t] = b
        start_smem[t] = off
        here = lane1 == t
        stv = jnp.where(here, off.astype(f32), stv)
        env = jnp.where(here, (off + n).astype(f32), env)
        bnv = jnp.where(here, b.astype(f32), bnv)
        off = off + n
    nb = b + 1
    nsup = (nb + 1) // 2

    ri = iota((SL, SL), 0)
    ci = iota((SL, SL), 1)
    o_all = o_ref[...].astype(bf16)
    tri_u = jnp.where(ri < ci, 1.0, 0.0) - jnp.where(ri == ci, 256.0, 0.0)
    pp_scr[...] = nn_dot(o_all, tri_u.astype(bf16))
    same_blk = (ri // 16) == (ci // 16)
    tri_b = jnp.where(same_blk & (ri < ci), 1.0, 0.0).astype(bf16)
    r32 = iota((NT, NT), 0)
    c32 = iota((NT, NT), 1)
    before = nn_dot(jnp.where(c32 < r32, 1.0, 0.0).astype(bf16), o_all)
    base, at = [], 0
    for c in caps:
        base.append(at)
        at += c
    lane_blk = iota((NT, SL), 1) // 16
    base_v = jnp.zeros((NT, SL), f32)
    for j in range(8):
        base_v = jnp.where(lane_blk == j, float(base[j]), base_v)
    srcv = base_v + 1.0 + nn_dot(o_all, tri_b) + nn_dot(before.astype(bf16), jnp.where(same_blk, 1.0, 0.0).astype(bf16))
    hi = jnp.floor(srcv * (1.0 / 256.0)) * 256.0
    hilo_scr[:, :SL] = hi
    hilo_scr[:, SL:] = srcv - hi

    rif = ri.astype(f32)

    def pack(t, _):
        bt = bin_smem[t]
        st = start_smem[t]
        row = pp_scr[pl.ds(t, 1), :] + (st + 256).astype(f32)
        p = jnp.where(rif == row, 1.0, 0.0).astype(bf16)
        xp = nn_dot(p, tok_ref[t])
        p2 = jnp.concatenate([p, p], axis=1)
        hl = hilo_scr[pl.ds(t, 1), :]
        sp = nt_dot(p2, jnp.broadcast_to(hl, (SL, 2 * SL)).astype(bf16))
        st8 = nt_dot(jnp.broadcast_to(hl, (16, 2 * SL)).astype(bf16), p2)[:8]

        @pl.when(st == 0)
        def _():
            x_scr[bt] = xp
            src_scr[bt] = sp
            srct_scr[bt] = st8

        @pl.when(st != 0)
        def _():
            x_scr[bt] += xp
            src_scr[bt] += sp
            srct_scr[bt] += st8

        return 0

    @pl.when(nb % 2 == 1)
    def _():
        x_scr[nb] = jnp.zeros((SL, D), f32)
        src_scr[nb] = jnp.zeros((SL, SL), f32)
        srct_scr[nb] = jnp.zeros((8, SL), f32)

    lax.fori_loop(0, NT, pack, 0)

    gw_scr[...] = jnp.zeros_like(gw_scr)
    gwd_scr[...] = jnp.zeros_like(gwd_scr)
    sums_scr[...] = jnp.zeros_like(sums_scr)
    bup_scr[...] = jnp.zeros_like(bup_scr)
    s_ref[...] = jnp.zeros_like(s_ref)

    gain1, gain2 = sm_ref[64:65, :], sm_ref[65:66, :]
    shift1, shift2 = sm_ref[66:67, :], sm_ref[67:68, :]
    bq, bv, bo, bd = (sm_ref[68 + k : 69 + k, :] for k in range(4))
    M = 2 * SL
    lane128 = iota((SL, SL), 1)
    head0 = lane128 < 64
    zero_b = jnp.zeros((SL, SL), bf16)
    ind2 = jnp.concatenate([jnp.where(head0, 1.0, 0.0), jnp.where(head0, 0.0, 1.0)], axis=0).astype(bf16)

    def two(a):
        return jnp.concatenate([jnp.where(head0, a, zero_b), jnp.where(head0, zero_b, a)], axis=0)

    def body(s, _):
        b0 = 2 * s
        x = jnp.concatenate([x_scr[b0], x_scr[b0 + 1]], axis=0)
        mean = jnp.mean(x, axis=1, keepdims=True)
        cen = x - mean
        r1 = lax.rsqrt(jnp.mean(cen * cen, axis=1, keepdims=True) + EPS)
        xh1 = cen * r1
        nf = (xh1 * gain1 + shift1).astype(bf16)
        qkv_scr[:, :D] = ((nn_dot(nf, w_ref[:, :D]) + bq).astype(bf16) * jnp.asarray(0.125, bf16))
        qkv_scr[:, D:2 * D] = nn_dot(nf, w_ref[:, D:2 * D]).astype(bf16)
        qkv_scr[:, 2 * D:3 * D] = (nn_dot(nf, w_ref[:, 2 * D:3 * D]) + bv).astype(bf16)
        saved = []
        att_rows = []
        for h in range(2):
            rows = slice(h * SL, (h + 1) * SL)
            bf_ = (b0 + h).astype(f32)
            e_seg = jnp.where((rif >= stv) & (rif < env) & (bnv == bf_), 1.0, 0.0)
            ke = ((e_seg - 1.0) * BIG).astype(bf16)
            e_seg = e_seg.astype(bf16)
            ke2 = jnp.concatenate([ke, ke], axis=0)
            cols = []
            for p in range(2):
                q = qkv_scr[rows, p * SL:(p + 1) * SL]
                k = qkv_scr[rows, D + p * SL:D + (p + 1) * SL]
                v = qkv_scr[rows, 2 * D + p * SL:2 * D + (p + 1) * SL]
                k2, v2 = two(k), two(v)
                qx = jnp.concatenate([q, e_seg], axis=1)
                kx = jnp.concatenate([k2, ke2], axis=1)
                sc = nt_dot(qx, kx)
                m0 = jnp.max(sc[:, :SL], axis=1, keepdims=True)
                m1 = jnp.max(sc[:, SL:], axis=1, keepdims=True)
                e = jnp.concatenate([jnp.exp(sc[:, :SL] - m0), jnp.exp(sc[:, SL:] - m1)], axis=1).astype(bf16)
                y = nn_dot(e, jnp.concatenate([v2, ind2], axis=1))
                rinv = 1.0 / y[:, SL:]
                att = y[:, :SL] * rinv
                cols.append(att)
                saved.append((e, rinv, att))
            att_rows.append(jnp.concatenate(cols, axis=1))
        att = jnp.concatenate(att_rows, axis=0).astype(bf16)
        mixed = x + nn_dot(att, w_ref[:, 3 * D:4 * D]) + bo
        mean = jnp.mean(mixed, axis=1, keepdims=True)
        cen = mixed - mean
        r2 = lax.rsqrt(jnp.mean(cen * cen, axis=1, keepdims=True) + EPS)
        xh2 = cen * r2
        ns = (xh2 * gain2 + shift2).astype(bf16)

        srcm = jnp.concatenate([src_scr[b0], src_scr[b0 + 1]], axis=0)
        lane_m = iota((M, SL), 1).astype(f32)
        ge = jnp.zeros((M, D), f32)
        for c0 in range(0, rtot, 256):
            cw = min(256, rtot - c0)
            oh = [jnp.where(srcm[:, :w] == lane_m[:, :w] + float(c0 + c1 + 1), 1.0, 0.0)
                  for c1 in range(0, cw, SL) for w in [min(SL, cw - c1)]]
            oh = jnp.concatenate(oh, axis=1).astype(bf16)
            ge = ge + nn_dot(oh, r_ref[c0:c0 + cw, :])
        ge_b = ge.astype(bf16)

        enc = mixed + bd
        gns = jnp.zeros((M, D), f32)
        for c in range(4):
            cs = slice(c * D, (c + 1) * D)
            ws = slice(4 * D + c * D, 5 * D + c * D)
            wup = w_ref[:, ws]
            wdn = wd_ref[cs, :]
            v = nn_dot(ns, wup) + sm_ref[UP + c : UP + c + 1, :]
            vv = v * v
            a = 0.5 * jnp.tanh(v * (vv * (GELU_A * GELU_B) + GELU_A)) + 0.5
            hact = v * a
            dg = a + hact * (1.0 - a) * (vv * (6.0 * GELU_A * GELU_B) + 2.0 * GELU_A)
            hb = hact.astype(bf16)
            enc = enc + nn_dot(hb, wdn)
            gh = (nt_dot(ge_b, wdn) * dg)
            ghb = gh.astype(bf16)
            bup_scr[:, cs] += fold8(ghb.astype(f32))
            gns = gns + nt_dot(ghb, wup)
            gw_scr[:, ws] += tn_dot(ns, ghb)
            gwd_scr[:, cs] += tn_dot(ge_b, hb)
        encb = enc.astype(bf16)
        srow = jnp.concatenate([srct_scr[b0][:1], srct_scr[b0 + 1][:1]], axis=1)
        for c0 in range(0, rtot, 256):
            cw = min(256, rtot - c0)
            oht = jnp.where(iota((cw, M), 0).astype(f32) + float(c0 + 1) == srow, 1.0, 0.0).astype(bf16)
            s_ref[c0:c0 + cw, :] += nn_dot(oht, encb).astype(bf16)

        sums_scr[7] += fold8(ge)
        sums_scr[1] += fold8(gns * xh2)
        sums_scr[3] += fold8(gns)
        eg = gns * gain2
        gmix = ge + r2 * (eg - jnp.mean(eg, axis=1, keepdims=True) - xh2 * jnp.mean(eg * xh2, axis=1, keepdims=True))
        gao = gmix.astype(bf16)
        sums_scr[6] += fold8(gao.astype(f32))
        gw_scr[:, 3 * D:4 * D] += tn_dot(att, gao)
        gatt = nt_dot(gao, w_ref[:, 3 * D:4 * D])
        for h in range(2):
            rows = slice(h * SL, (h + 1) * SL)
            bf_ = (b0 + h).astype(f32)
            e_seg = jnp.where((rif >= stv) & (rif < env) & (bnv == bf_), 1.0, 0.0)
            ke = ((e_seg - 1.0) * BIG).astype(bf16)
            e_seg = e_seg.astype(bf16)
            e_seg2 = jnp.concatenate([e_seg, e_seg], axis=0)
            for p in range(2):
                q = qkv_scr[rows, p * SL:(p + 1) * SL]
                k = qkv_scr[rows, D + p * SL:D + (p + 1) * SL]
                v = qkv_scr[rows, 2 * D + p * SL:2 * D + (p + 1) * SL]
                k2, v2, q2 = two(k), two(v), two(q)
                e, rinv, at_ = saved[2 * h + p]
                da = gatt[rows, p * SL:(p + 1) * SL] * rinv
                dao = (da * at_).astype(bf16)
                da = da.astype(bf16)
                dp = nt_dot(jnp.concatenate([da, dao], axis=1), jnp.concatenate([v2, -ind2], axis=1))
                gsc = (e.astype(f32) * dp).astype(bf16)
                gq = nn_dot(gsc, k2) * 0.125
                da2, dao2 = two(da), two(dao)
                st_ = nt_dot(jnp.concatenate([k, ke], axis=1), jnp.concatenate([q2, e_seg2], axis=1))
                et = jnp.exp(st_ - jnp.max(st_, axis=0, keepdims=True)).astype(bf16)
                dpt = nt_dot(jnp.concatenate([v, jnp.full((SL, SL), -1.0, bf16)], axis=1), jnp.concatenate([da2, dao2], axis=1))
                gst = (et.astype(f32) * dpt).astype(bf16)
                gv = nn_dot(et, da2)
                gk = nn_dot(gst, q2)
                gqkv_scr[rows, p * SL:(p + 1) * SL] = gq.astype(bf16)
                gqkv_scr[rows, D + p * SL:D + (p + 1) * SL] = gk.astype(bf16)
                gqkv_scr[rows, 2 * D + p * SL:2 * D + (p + 1) * SL] = gv.astype(bf16)
        gqkv = gqkv_scr[...]
        sums_scr[4] += fold8(gqkv[:, :D].astype(f32))
        sums_scr[5] += fold8(gqkv[:, 2 * D:].astype(f32))
        gw_scr[:, :3 * D] += tn_dot(nf, gqkv)
        gnf = nt_dot(gqkv, w_ref[:, :3 * D])
        sums_scr[0] += fold8(gnf * xh1)
        sums_scr[2] += fold8(gnf)
        eg = gnf * gain1
        gtok = gmix + r1 * (eg - jnp.mean(eg, axis=1, keepdims=True) - xh1 * jnp.mean(eg * xh1, axis=1, keepdims=True))
        for h in range(2):
            part = gtok[h * SL:(h + 1) * SL]
            hi_ = part.astype(bf16)
            g_scr[b0 + h, :SL, :] = hi_
            g_scr[b0 + h, SL:, :] = (part - hi_.astype(f32)).astype(bf16)
        return 0

    lax.fori_loop(0, nsup, body, 0)

    tri_l = (jnp.where(ci < ri, 1.0, 0.0) - jnp.where(ri == ci, 256.0, 0.0)).astype(bf16)
    cif = ci.astype(f32)

    def unpack(t, _):
        bt = bin_smem[t]
        st = start_smem[t]
        col = nt_dot(tri_l, jnp.broadcast_to(o_ref[pl.ds(t, 1), :], (SL, SL)).astype(bf16))
        pt = jnp.where(col + (st + 256).astype(f32) == cif, 1.0, 0.0).astype(bf16)
        gtok_ref[t] = nn_dot(jnp.concatenate([pt, pt], axis=1), g_scr[bt])
        return 0

    lax.fori_loop(0, NT, unpack, 0)

    fin = [jnp.sum(sums_scr[k], axis=0, keepdims=True) for k in range(8)]
    gsm = jnp.concatenate([gpart_ref[:64, :]] + fin + [gpart_ref[72:73, :], jnp.zeros((55, D), f32)], axis=0).astype(bf16)
    eye = jnp.where(iota((D, D), 0) == iota((D, D), 1), 1.0, 0.0).astype(bf16)
    smt = nt_dot(eye, gsm)
    bup = jnp.sum(bup_scr[...], axis=0, keepdims=True).astype(bf16)
    dsel = iota((SL, FF), 0) == iota((SL, FF), 1) // 8
    bup_m = jnp.where(dsel, jnp.broadcast_to(bup, (SL, FF)), jnp.zeros((SL, FF), bf16))
    rep = jnp.where(iota((SL, FF), 0) == 80 + iota((SL, FF), 1) % 8, 1.0, 0.0).astype(bf16)
    bup_d = nt_dot(bup_m, rep)
    even = jnp.where(iota((D, SL), 0) == 2 * iota((D, SL), 1), 1.0, 0.0).astype(bf16)
    smt = (smt + nn_dot(even, bup_d.astype(bf16))).astype(bf16)
    gwd_t = [nt_dot(eye, gwd_scr[:, c * D:(c + 1) * D].astype(bf16)).astype(bf16) for c in range(4)]
    pr = iota((D, D), 0)
    pc = iota((D, D), 1)
    pd, prr = pr // 32, pr % 32
    want = jnp.where(prr < 18, (prr % 9) * 16 + pd * 2 + prr // 9, jnp.where(prr < 26, 144 + pd * 8 + prr - 18, -1))
    perm = jnp.where(want == pc, 1.0, 0.0).astype(bf16)
    sm_pad = jnp.zeros((16, SL), bf16)
    tail = jnp.zeros((48, D), bf16)
    for qn in range(16):
        r16 = slice(qn * 16, qn * 16 + 16)
        parts = [gw_scr[r16, bb * D:(bb + 1) * D].astype(bf16) for bb in range(8)]
        parts.append(jnp.concatenate([smt[r16], sm_pad], axis=1))
        o = (qn % 4) * 64
        parts.append(gwd_t[qn // 4][o:o + 64])
        parts.append(tail)
        gs_ref[qn] = nn_dot(perm, jnp.concatenate(parts, axis=0)).astype(bf16)


def encoder(caps, nt, o32, tok, w, wd, sm, r, gpart):
    rtot = sum(caps)
    vm = pl.BlockSpec(memory_space=pltpu.VMEM)
    return pl.pallas_call(
        functools.partial(encoder_kernel, caps),
        out_shape=(jax.ShapeDtypeStruct((NT, SL, D), f32), jax.ShapeDtypeStruct((rtot, D), bf16),
                   jax.ShapeDtypeStruct((16, D, D), bf16)),
        in_specs=[pl.BlockSpec(memory_space=pltpu.SMEM)] + [vm] * 7,
        out_specs=(vm, vm, vm),
        scratch_shapes=[
            pltpu.VMEM((NT, SL, D), f32), pltpu.VMEM((NT, SL, SL), f32), pltpu.VMEM((NT, 8, SL), f32),
            pltpu.VMEM((NT, 2 * SL, D), bf16), pltpu.VMEM((D, 2048), f32), pltpu.VMEM((D, FF), f32),
            pltpu.VMEM((8, 8, D), f32), pltpu.VMEM((8, FF), f32), pltpu.VMEM((NT, SL), f32),
            pltpu.VMEM((2 * SL, 768), bf16), pltpu.VMEM((2 * SL, 768), bf16), pltpu.VMEM((NT, 2 * SL), f32),
            pltpu.SMEM((NT,), i32), pltpu.SMEM((NT,), i32),
        ],
        compiler_params=pltpu.CompilerParams(vmem_limit_bytes=VMEM_LIMIT),
        name="encoder_fwd_bwd",
    )(nt, o32, tok, w, wd, sm, r, gpart)


def scatter_kernel(
    caps, gs_ref, s_ref, slab_out, rows_out,
    got1, sum1, got2, sum2, got3, sum3, got4, s_sem, r_sem, s1, r1, s2, r2, s3, r3, s4, r4, own_sem,
):
    me = Place()
    base = bases(caps)
    most, room = decode_room(caps)
    for i in range(8):
        rows_out[i] = jnp.zeros((room, D), bf16)
    barrier, count = me.greet()
    pl.semaphore_wait(barrier, count)

    step1 = []
    for x in (1, 3, 0, 2):
        c = remote(gs_ref.at[x, 1 - me.core], got1.at[x], s1.at[x], r1.at[x], me.sibling())
        c.start()
        step1.append((x, c))
    for k in (4, 3, 5, 2, 6, 1, 7, 0):
        for j in range(8):
            part = s_ref.at[pl.ds(base[j], caps[j])]
            there = rows_out.at[me.seq, pl.ds(0, caps[j])]
            if k == 0:
                @pl.when(me.seq == j)
                def _():
                    pltpu.make_async_copy(part, there, own_sem).start()
            else:
                @pl.when((me.seq + k) % 8 == j)
                def _():
                    remote(part, there, s_sem.at[k], r_sem.at[k], me.seq_peer(k)).start()

    for x, c in step1:
        c.wait()
        for z in range(4):
            for y in range(4):
                total = gs_ref[x, me.core, 4 * z + y].astype(f32) + got1[x, 4 * z + y].astype(f32)
                if x < 2:
                    sum1[0, z, x % 2, y] = total.astype(bf16)
                else:
                    sum1[1, y, x % 2, z] = total.astype(bf16)
    first = (me.z, me.y)
    second = (me.y, me.z)
    peers = (me.z_peer, me.y_peer)
    step2 = []
    for k in (2, 1, 3):
        for h in range(2):
            c = remote(sum1.at[h, (first[h] + k) % 4], got2.at[h, k - 1], s2.at[h, k - 1], r2.at[h, k - 1], peers[h](k))
            c.start()
            step2.append(c)
    for c in step2:
        c.wait()
    for h in range(2):
        for x2 in range(2):
            for o in range(4):
                total = sum1[h, first[h], x2, o].astype(f32)
                for k in range(3):
                    total = total + got2[h, k, x2, o].astype(f32)
                sum2[h, o, x2] = total.astype(bf16)
    step3 = []
    for k in (2, 1, 3):
        for h in range(2):
            c = remote(sum2.at[h, (second[h] + k) % 4], got3.at[h, k - 1], s3.at[h, k - 1], r3.at[h, k - 1], peers[1 - h](k))
            c.start()
            step3.append(c)
    for c in step3:
        c.wait()
    for h in range(2):
        for x2 in range(2):
            total = sum2[h, second[h], x2].astype(f32)
            for k in range(3):
                total = total + got3[h, k, x2].astype(f32)
            sum3[2 * h + x2] = total.astype(bf16)
    step4 = []
    for k in (2, 1, 3):
        c = remote(sum3.at[(me.x + k) % 4], got4.at[k - 1], s4.at[k - 1], r4.at[k - 1], me.x_peer(k))
        c.start()
        step4.append(c)
    for c in step4:
        c.wait()
    total = sum3[me.x].astype(f32)
    for k in range(3):
        total = total + got4[k].astype(f32)
    slab_out[...] = total

    for j in range(8):
        @pl.when(me.seq == j)
        def _():
            here = rows_out.at[0, pl.ds(0, caps[j])]
            for k in range(1, 8):
                pltpu.make_async_copy(here, here, r_sem.at[k]).wait()
            pltpu.make_async_copy(here, here, own_sem).wait()
            for k in range(1, 8):
                there = s_ref.at[pl.ds(base[(j + k) % 8], caps[(j + k) % 8])]
                pltpu.make_async_copy(there, there, s_sem.at[k]).wait()


def scatter(caps, gs, s, cid):
    dma = pltpu.SemaphoreType.DMA
    most, room = decode_room(caps)
    return pl.pallas_call(
        functools.partial(scatter_kernel, caps),
        out_shape=(jax.ShapeDtypeStruct((32, D), f32), jax.ShapeDtypeStruct((8, room, D), bf16)),
        in_specs=[vmem()] * 2,
        out_specs=(vmem(),) * 2,
        scratch_shapes=[
            pltpu.VMEM((4, 16, 32, D), bf16), pltpu.VMEM((2, 4, 2, 4, 32, D), bf16),
            pltpu.VMEM((2, 3, 2, 4, 32, D), bf16), pltpu.VMEM((2, 4, 2, 32, D), bf16),
            pltpu.VMEM((2, 3, 2, 32, D), bf16), pltpu.VMEM((4, 32, D), bf16), pltpu.VMEM((3, 32, D), bf16),
            dma((8,)), dma((8,)), dma((4,)), dma((4,)), dma((2, 3)), dma((2, 3)), dma((2, 3)), dma((2, 3)),
            dma((3,)), dma((3,)), dma,
        ],
        compiler_params=pltpu.CompilerParams(collective_id=cid, has_side_effects=True, vmem_limit_bytes=VMEM_LIMIT),
        name="scatter_and_exchange",
    )(gs, s)


def decode_kernel(
    caps, len_ref, vis_ref, rows_ref, sm_ref, slab_ref,
    dec_out, gain_out, shift_out, wq_out, wo_out, wu_out, wd_out, bias_out, up_out, mask_out, te_out,
    rows_scr,
):
    seq = lax.axis_index("seq")
    most, room = decode_room(caps)
    valid, shown = mask_rows(len_ref, vis_ref)
    v8, s8 = part_lanes(valid, shown, seq)
    stack = jnp.concatenate(
        [part_ranks(v8 * s8), v8 * (1.0 - s8), v8, jnp.zeros((SL - 24, PART), f32)], axis=0
    )
    cols = stack.T
    steps = sm_ref[pl.ds(pl.multiple_of(TE + 8 * seq, 8), 8), :]
    extra = jnp.concatenate([sm_ref[MASK : MASK + 1, :], steps, jnp.zeros((7, D), f32)], axis=0).astype(bf16)
    lane = iota((PART, room), 1)
    step_lane = most + 1 + (iota((PART, room), 0) % 16) // 2
    lane_rank = (lane - PART).astype(f32)
    for i in range(8):
        hit = (cols[:, i : i + 1] == lane_rank) & (lane < most)
        hidden = (lane == most) & (cols[:, 8 + i : 9 + i] > 0.0)
        timed = (lane == step_lane) & (cols[:, 16 + i : 17 + i] > 0.0)
        lhs = one_zero(hit | hidden | timed).astype(bf16)
        rows_scr[...] = rows_ref[i]
        rows_scr[most : most + 16, :] = extra
        got = nn_dot(lhs, rows_scr[...]).astype(bf16)
        dec_out[:, 8 * i : 8 * i + 8] = got.reshape(MICRO, 8, 16, D)

    slab = slab_ref[...]
    r, c = iota((SL, SL), 0), iota((SL, SL), 1)
    small = []
    for f in range(2):
        one = slice(f, f + 1)
        for b in range(3):
            wq_out[one, b * D : (b + 1) * D] = slab[9 * f + b : 9 * f + b + 1]
        wo_out[one, :] = slab[9 * f + 3 : 9 * f + 4]
        for b in range(4):
            wu_out[one, b * D : (b + 1) * D] = slab[9 * f + 4 + b : 9 * f + 5 + b]
        row = jnp.broadcast_to(slab[9 * f + 8 : 9 * f + 9, :SL], (SL, SL))
        small.append(jnp.sum(jnp.where(r == c, row, 0.0), axis=1, keepdims=True))
    wd_out[...] = slab[18:26]
    small = jnp.concatenate(small, axis=1)
    te_out[...] = small[TE : TE + 64]
    gain_out[...] = small[GAIN : GAIN + 2]
    shift_out[...] = small[SHIFT : SHIFT + 2]
    bias_out[...] = small[BIAS : BIAS + 4]
    mask_out[...] = small[MASK : MASK + 1]
    up_out[...] = slab[8:9, UP : UP + 8]


def decode(caps, lengths, visible, rows, sm, slab):
    most, room = decode_room(caps)
    s = jax.ShapeDtypeStruct
    return pl.pallas_call(
        functools.partial(decode_kernel, caps),
        out_shape=(
            s((MICRO, TRAJ, 16, D), bf16), s((2, 2), f32), s((2, 2), f32), s((2, 3 * D), f32), s((2, D), f32),
            s((2, FF), f32), s((8, D), f32), s((4, 2), f32), s((1, 8), f32), s((1, 2), f32), s((64, 2), f32),
        ),
        in_specs=[vmem()] * 5,
        out_specs=(vmem(),) * 11,
        scratch_shapes=[pltpu.VMEM((room, D), bf16)],
        compiler_params=pltpu.CompilerParams(vmem_limit_bytes=VMEM_LIMIT),
        name="decode",
    )(lengths, visible, rows, sm, slab)


def per_device(
    tokens, lengths, visible, norm_gains, norm_biases, w_qkv, w_out, w_up, w_down, proj_biases, up_bias, mask_token,
    time_embed, dec_grad,
):
    lengths, visible = lengths[:, 0], visible[:, 0]
    tok = tokens.reshape(NT, SL, D)
    dg = dec_grad[:, 0]
    small = jnp.concatenate(
        [time_embed.T, norm_gains.T, norm_biases.T, proj_biases.T, mask_token[:, None], jnp.zeros((2, 7), bf16)], axis=1
    )
    ups = jnp.concatenate([up_bias[None], jnp.zeros((1, 8), bf16)], axis=0)
    small = jnp.concatenate([small, ups, jnp.zeros((2, 40), bf16)], axis=1)
    w, wd, sm, rows, opened, counts, sums = gather(
        CAPS, lengths, visible, dg, w_qkv, w_out, w_up, w_down, small, 0
    )

    def rest(caps, rows, cid):
        gtok, s, gs = encoder(caps, counts, opened, tok, w, wd, sm, rows, sums)
        slab, back = scatter(caps, gs.reshape(4, 2, 16, 32, D), s, cid)
        return (gtok,) + tuple(decode(caps, lengths, visible, back, sm, slab))

    def roomy():
        return rest(FULL, exchange(FULL, lengths, visible, dg, 1), 2)

    outs = lax.cond(jnp.max(sm[FLAG]) > 0.0, roomy, lambda: rest(CAPS, rows, 3))
    gtok, dec, gain, shift, wq, wo, wu, wdn, bias, up, mask, te = outs
    return (
        dec.reshape(MICRO, 1, TRAJ, 16, D), gtok.reshape(MICRO, 1, 8, SL, D), gain, shift, wq, wo, wu, wdn, bias,
        up.reshape(8), mask.reshape(2), te,
    )


def solution(mesh):
    everyone = ("seq", "dp")
    return jax.shard_map(
        per_device,
        mesh=mesh,
        in_specs=(
            P(None, "dp", "seq", None, None), P(None, "dp", None), P(None, "dp", None, None), P(None, everyone),
            P(None, everyone), P(everyone, None), P(everyone, None), P(everyone, None), P(everyone, None),
            P(None, everyone), P(everyone), P(everyone), P(None, everyone), P(None, "dp", None, "seq", None),
        ),
        out_specs=(
            P(None, "dp", None, "seq", None), P(None, "dp", "seq", None, None), P(None, everyone), P(None, everyone),
            P(everyone, None), P(everyone, None), P(everyone, None), P(everyone, None), P(None, everyone), P(everyone),
            P(everyone), P(None, everyone),
        ),
        check_vma=False,
    )
```

```python
import functools

import jax
import jax.numpy as jnp
from jax import lax
from jax.experimental import pallas as pl
from jax.experimental.pallas import tpu as pltpu
from jax.sharding import PartitionSpec as P

f32, bf16, i32 = jnp.float32, jnp.bfloat16, jnp.int32
EPS = 1e-5
BIG = 1e30
D, FF, SL, MICRO, TRAJ = 256, 1024, 128, 4, 64
NT = 32
PART = 512
GELU_A = 0.7978845608028654
GELU_B = 0.044715
CAPS, NBINS = (304, 240, 192, 160, 128, 80, 64, 48), 8
FULL, NFULL = (PART,) * 8, NT
MESH = pl.DeviceIdType.MESH
VMEM_LIMIT = 30 * 2**20
VMEM_MOST = 56 * 2**20

TE, GAIN, SHIFT, BIAS, MASK, UP, FLAG = 0, 64, 66, 68, 72, 80, 96


def nt_dot(a, b):
    return lax.dot_general(a, b, (((1,), (1,)), ((), ())), preferred_element_type=f32)


def nn_dot(a, b):
    return lax.dot_general(a, b, (((1,), (0,)), ((), ())), preferred_element_type=f32)


def tn_dot(a, b):
    return lax.dot_general(a, b, (((0,), (0,)), ((), ())), preferred_element_type=f32)


def iota(shape, dim):
    return lax.broadcasted_iota(i32, shape, dim)


def one_zero(cond):
    return jnp.where(cond, 1.0, 0.0)


def fold8(v):
    n = v.shape[0] // 8
    return jnp.sum(v.reshape(n, 8, v.shape[1]), axis=0)


def bases(caps):
    out, at = [], 0
    for c in caps:
        out.append(at)
        at += c
    return out


def decode_room(caps):
    most = max(caps)
    return most, -(-(most + 16) // SL) * SL


class Place:
    def __init__(self):
        self.seq = lax.axis_index("seq")
        self.dp = lax.axis_index("dp")
        self.x, self.core = self.seq // 2, self.seq % 2
        self.z, self.y = self.dp // 4, self.dp % 4

    def at(self, x, y, z):
        return (2 * x + self.core, z * 4 + y)

    def seq_peer(self, k):
        return ((self.seq + k) % 8, self.dp)

    def y_peer(self, k):
        return self.at(self.x, (self.y + k) % 4, self.z)

    def z_peer(self, k):
        return self.at(self.x, self.y, (self.z + k) % 4)

    def sibling(self):
        return (self.seq + 1 - 2 * self.core, self.dp)

    def greet(self, everyone=True):
        peers = [self.seq_peer(k) for k in range(1, 8)]
        if everyone:
            for dx in range(4):
                for d in range(1, 4):
                    peers.append(self.at((self.x + dx) % 4, (self.y + d) % 4, self.z))
                    peers.append(self.at((self.x + dx) % 4, self.y, (self.z + d) % 4))
        barrier = pltpu.get_barrier_semaphore()
        for peer in peers:
            pl.semaphore_signal(barrier, inc=1, device_id=peer, device_id_type=MESH)
        return barrier, len(peers)


def remote(src, dst, send_sem, recv_sem, peer):
    return pltpu.make_async_remote_copy(
        src_ref=src, dst_ref=dst, send_sem=send_sem, recv_sem=recv_sem, device_id=peer, device_id_type=MESH
    )


def arrived(ref, sem):
    pltpu.make_async_copy(ref, ref, sem).wait()


def vmem():
    return pl.BlockSpec(memory_space=pltpu.VMEM)


def hbm():
    return pl.BlockSpec(memory_space=pltpu.HBM)


def smem():
    return pl.BlockSpec(memory_space=pltpu.SMEM)


def mask_rows(len_ref, vis_ref):
    eye = one_zero(iota((TRAJ, TRAJ), 0) == iota((TRAJ, TRAJ), 1)).astype(bf16)
    step = (iota((TRAJ, SL), 1) // 2).astype(f32)
    valid, shown = [], []
    for m in range(MICRO):
        row = jnp.broadcast_to(len_ref[m : m + 1, :].astype(f32), (SL, TRAJ)).astype(bf16)
        valid.append(one_zero(step < nt_dot(eye, row)))
        shown.append(one_zero(vis_ref[m] > 0))
    return jnp.concatenate(valid, axis=0), jnp.concatenate(shown, axis=0)


def part_lanes(valid, shown, part):
    n = MICRO * TRAJ
    pick = one_zero(iota((SL, PART), 0) == 16 * part + iota((SL, PART), 1) % 16).astype(bf16)
    row, lane = iota((n, PART), 0), iota((n, PART), 1)
    mine = (row // TRAJ == lane // SL) & (row % 8 == (lane % SL) // 16)
    group = one_zero((iota((16, n), 1) % TRAJ) // 8 == iota((16, n), 0)).astype(bf16)

    def lanes(mask):
        spread = nn_dot(mask.astype(bf16), pick)
        return nn_dot(group, jnp.where(mine, spread, 0.0).astype(bf16))[:8]

    return lanes(valid), lanes(shown)


def part_ranks(open_lanes):
    tri = one_zero(iota((PART, PART), 0) < iota((PART, PART), 1)).astype(bf16)
    rows = jnp.concatenate([open_lanes, jnp.zeros((8, PART), f32)], axis=0).astype(bf16)
    return nn_dot(rows, tri)[:8]


def prepare_part(caps, seq, valid, shown, rank_scr, ext_scr, cols_out):
    most, _ = decode_room(caps)
    v8, s8 = part_lanes(valid, shown, seq)
    rank = part_ranks(v8 * s8)
    rank_scr[...] = jnp.where(v8 * s8 > 0.0, rank, -1.0)
    lane_step = (iota((8, PART), 1) % 16) // 2
    step_row = iota((8, PART), 0)
    for i in range(8):
        v = v8[i : i + 1, :]
        steps = jnp.where(lane_step == step_row, jnp.broadcast_to(v, (8, PART)), 0.0)
        hidden = jnp.where(step_row == 0, jnp.broadcast_to(v * (1.0 - s8[i : i + 1, :]), (8, PART)), 0.0)
        ext_scr[i] = jnp.concatenate([steps, hidden], axis=0)
    first = jnp.where(v8 > 0.0, jnp.where(s8 > 0.0, rank, float(most)), -1.0)
    second = jnp.where(v8 > 0.0, (most + 1 + lane_step).astype(f32), -1.0)
    cols_out[...] = jnp.concatenate([first, second, jnp.zeros((SL - 16, PART), f32)], axis=0).T


def plan_bins(caps, nbins, opened, base_scr, bin_scr, pos_scr, srct_scr, seg_out, bins_out, count_out, slot_out):
    n_rep = nn_dot(opened.astype(bf16), jnp.ones((SL, SL), bf16))
    at = [jnp.full((1, SL), float(k), f32) for k in range(3)]
    used = [jnp.zeros((1, SL), f32) for _ in range(3)]
    last = jnp.zeros((1, SL), f32)
    for t in range(NT):
        n = n_rep[t : t + 1]
        fits = [u + n <= float(SL) for u in used]
        none = jnp.logical_not(fits[0] | fits[1] | fits[2])
        used = [jnp.where(none, u, v) for u, v in zip(used[1:] + [jnp.zeros((1, SL), f32)], used)]
        at = [jnp.where(none, a, b) for a, b in zip(at[1:] + [at[2] + 1.0], at)]
        take = [fits[0], fits[1] & jnp.logical_not(fits[0])]
        take.append(jnp.logical_not(take[0] | take[1]))
        bin_now = jnp.where(take[0], at[0], jnp.where(take[1], at[1], at[2]))
        off = jnp.where(take[0], used[0], jnp.where(take[1], used[1], used[2]))
        used = [jnp.where(f, u + n, u) for f, u in zip(take, used)]
        last = jnp.maximum(last, bin_now)
        base_scr[t : t + 1, :] = bin_now * float(SL) + off
        bin_scr[t : t + 1, :] = bin_now
    ri, ci = iota((SL, SL), 0), iota((SL, SL), 1)
    within = nn_dot(opened.astype(bf16), one_zero(ri < ci).astype(bf16))
    base, bins = base_scr[...], bin_scr[...]
    pos = jnp.where(opened > 0.0, base + within, -1.0)
    pos_scr[...] = pos
    pad = jnp.zeros((SL - NT, SL), f32)
    slot_out[...] = jnp.concatenate([jnp.where(opened > 0.0, pos - bins * float(SL), -1.0), pad], axis=0).T
    lo = jnp.concatenate([base, pad], axis=0).T[:8]
    hi = jnp.concatenate([base + n_rep, pad], axis=0).T[:8]
    seg_out[...] = jnp.where(iota((8, SL), 0) == 0, lo, hi)
    bins_out[...] = jnp.concatenate([bins, pad], axis=0).T[:8].astype(i32)
    count_out[...] = jnp.broadcast_to(last + 1.0, (8, SL)).astype(i32)
    same = ri // 16 == ci // 16
    first = bases(caps)
    lane_blk = iota((NT, SL), 1) // 16
    src = jnp.ones((NT, SL), f32)
    for j in range(8):
        src = jnp.where(lane_blk == j, float(first[j] + 1), src)
    before = nn_dot(one_zero(iota((NT, NT), 1) < iota((NT, NT), 0)).astype(bf16), opened.astype(bf16))
    src = src + nn_dot(opened.astype(bf16), one_zero(same & (ri < ci)).astype(bf16))
    src = src + nn_dot(before.astype(bf16), one_zero(same).astype(bf16))
    big = jnp.floor(src * (1.0 / 256.0)) * 256.0
    srct_scr[...] = jnp.concatenate([big, src - big, jnp.zeros((SL - 2 * NT, SL), f32)], axis=0).T.astype(bf16)
    return one_zero(last[:, :1] + 1.0 > float(nbins))


def pack_tokens(nbins, tok_ref, pos_scr, srct_scr, seg_out, src_scr, x_out, src_out):
    m = 2 * SL
    row = iota((m, SL), 0).astype(f32)
    row_low = iota((m, m), 0).astype(f32).astype(bf16)
    one, zero = jnp.ones((m, m), bf16), jnp.zeros((m, m), bf16)
    lo, hi = seg_out[0:1, :], seg_out[1:2, :]
    lo2 = jnp.concatenate([lo[:, :NT], lo[:, :NT], lo[:, 2 * NT :]], axis=1)
    hi2 = jnp.concatenate([hi[:, :NT], hi[:, :NT], hi[:, 2 * NT :]], axis=1)

    def pair(s, _):
        here = pl.ds(pl.multiple_of(s * m, m), m)
        at = row + (s * m).astype(f32)
        total = jnp.zeros((m, D), f32)
        slots = jnp.zeros((m, SL), bf16)
        for t in range(0, NT, 2):
            local = jnp.concatenate([pos_scr[t : t + 1, :], pos_scr[t + 1 : t + 2, :]], axis=1) - (s * m).astype(f32)
            local = jnp.where((local >= 0.0) & (local < float(m)), local, -1.0)
            p = jnp.where(row_low == jnp.broadcast_to(local, (m, m)).astype(bf16), one, zero)
            slots = slots + (p[:, :SL] + p[:, SL:])
            total = total + nn_dot(p, tok_ref[t : t + 2].reshape(m, D))
        x_out[here, :] = total.astype(bf16)
        seg = (at >= lo2) & (at < hi2)
        src = jnp.sum(jnp.where(seg, nn_dot(slots, srct_scr[...]), 0.0), axis=1, keepdims=True)
        src = jnp.broadcast_to(src, (m, SL))
        src_scr[here, :] = src
        src_out[pl.ds(pl.multiple_of(s * 16, 16), 16), :] = jnp.concatenate([src[:SL].T[:8], src[SL:].T[:8]], axis=0)
        return 0

    lax.fori_loop(0, nbins // 2, pair, 0)


def pack_received(caps, nbins, r_ref, src_scr, ge_out):
    total = sum(caps)
    m = 2 * SL
    lane = iota((m, SL), 1).astype(f32)

    def one(s, _):
        here = pl.ds(pl.multiple_of(s * m, m), m)
        src = src_scr[here, :]
        got = jnp.zeros((m, D), f32)
        for c in range(0, total, 256):
            wide = min(256, total - c)
            hit = [
                one_zero(src[:, :w] == lane[:, :w] + float(c + d + 1))
                for d in range(0, wide, SL) for w in [min(SL, wide - d)]
            ]
            got = got + nn_dot(jnp.concatenate(hit, axis=1).astype(bf16), r_ref[c : c + wide, :])
        ge_out[here, :] = got.astype(bf16)
        return 0

    lax.fori_loop(0, nbins // 2, one, 0)


def pack_part(caps, me, k, dg_ref, rank_scr, ext_scr, buf):
    most = max(caps)
    owner = (me.seq + k) % 8
    hit = one_zero(rank_scr[pl.ds(owner, 1), :] == iota((most, PART), 0).astype(f32))
    lhs = jnp.concatenate([hit, ext_scr[owner]], axis=0).astype(bf16)
    first = pl.multiple_of(owner * 8, 8)
    parts = [dg_ref[m, pl.ds(first, 8)].reshape(SL, D) for m in range(MICRO)]
    got = nn_dot(lhs, jnp.concatenate(parts, axis=0))
    buf[k] = got[:most].astype(bf16)
    return got[most:]


def send_parts(caps, me, buf, r_ref, sends, recvs):
    base = bases(caps)
    for j in range(8):
        @pl.when(me.seq == j)
        def _():
            there = r_ref.at[pl.ds(base[j], caps[j])]
            for k in (4, 3, 5, 2, 6, 1, 7):
                remote(buf.at[k, pl.ds(0, caps[j])], there, sends.at[k], recvs.at[j], me.seq_peer(k)).start()
            there[...] = buf[0, : caps[j]]


def finish_parts(caps, me, buf, r_ref, sends, recvs):
    base = bases(caps)
    for j in range(8):
        @pl.when(me.seq != j)
        def _():
            arrived(r_ref.at[pl.ds(base[j], caps[j])], recvs.at[j])

        @pl.when(me.seq == j)
        def _():
            for k in range(1, 8):
                arrived(buf.at[k, pl.ds(0, caps[j])], sends.at[k])


def part_scratch(caps, nbins):
    return [
        pltpu.VMEM((MICRO, TRAJ, 16, D), bf16),
        pltpu.VMEM((NT, SL, D), bf16),
        pltpu.SemaphoreType.DMA((2,)),
        pltpu.VMEM((MICRO * TRAJ, SL), f32),
        pltpu.VMEM((8, PART), f32),
        pltpu.VMEM((8, 16, PART), f32),
        pltpu.VMEM((8, max(caps), D), bf16),
        pltpu.VMEM((sum(caps), D), bf16),
        pltpu.SemaphoreType.DMA((8,)),
        pltpu.SemaphoreType.DMA((8,)),
        pltpu.VMEM((NT, SL), f32),
        pltpu.VMEM((NT, SL), f32),
        pltpu.VMEM((NT, SL), f32),
        pltpu.VMEM((SL, SL), bf16),
        pltpu.VMEM((nbins * SL, SL), f32),
    ]


def part_outs(caps, nbins):
    s = jax.ShapeDtypeStruct
    return (
        s((nbins * SL, D), bf16),
        s((nbins * SL, D), bf16),
        s((8, SL), f32),
        s((nbins * 8, SL), f32),
        s((SL, SL), f32),
        s((8, SL), i32),
        s((8, SL), i32),
        s((PART, SL), f32),
    )


class Parts:
    def __init__(self, caps, nbins, me, len_ref, vis_ref, dg_hbm, tok_hbm, outs, scratch):
        self.caps, self.nbins, self.me = caps, nbins, me
        self.len_ref, self.vis_ref, self.dg_hbm, self.tok_hbm = len_ref, vis_ref, dg_hbm, tok_hbm
        self.x, self.ge, self.seg, self.src, self.slot, self.bins, self.count, self.cols = outs
        (
            self.dg, self.tok, self.load_sem, self.open_scr, self.rank, self.ext, self.buf, self.r, self.sends,
            self.recvs, self.base_scr, self.bin_scr, self.pos, self.srct, self.src_scr,
        ) = scratch

    def load(self):
        self.loads = [
            pltpu.make_async_copy(self.dg_hbm, self.dg, self.load_sem.at[0]),
            pltpu.make_async_copy(self.tok_hbm, self.tok, self.load_sem.at[1]),
        ]
        for c in self.loads:
            c.start()

    def prepare(self):
        me = self.me
        valid, shown = mask_rows(self.len_ref, self.vis_ref)
        opened = valid * shown
        self.open_scr[...] = opened
        mine = [
            self.open_scr[pl.ds(pl.multiple_of(m * TRAJ + 8 * me.seq, 8), 8), :] for m in range(MICRO)
        ]
        over = plan_bins(
            self.caps, self.nbins, jnp.concatenate(mine, axis=0), self.base_scr, self.bin_scr, self.pos, self.srct,
            self.seg, self.bins, self.count, self.slot,
        )
        prepare_part(self.caps, me.seq, valid, shown, self.rank, self.ext, self.cols)
        return opened, over

    def send(self):
        sums = jnp.zeros((16, D), f32)
        for k in range(8):
            sums = sums + pack_part(self.caps, self.me, k, self.dg, self.rank, self.ext, self.buf)
        send_parts(self.caps, self.me, self.buf, self.r, self.sends, self.recvs)
        return sums

    def pack_tokens(self):
        pack_tokens(self.nbins, self.tok, self.pos, self.srct, self.seg, self.src_scr, self.x, self.src)

    def receive(self):
        finish_parts(self.caps, self.me, self.buf, self.r, self.sends, self.recvs)
        pack_received(self.caps, self.nbins, self.r, self.src_scr, self.ge)


def exchange_kernel(caps, nbins, len_ref, vis_ref, dg_hbm, tok_hbm, *refs):
    me = Place()
    barrier, count = me.greet(everyone=False)
    parts = Parts(caps, nbins, me, len_ref, vis_ref, dg_hbm, tok_hbm, refs[:8], refs[8:])
    parts.load()
    parts.prepare()
    for c in parts.loads:
        c.wait()
    pl.semaphore_wait(barrier, count)
    parts.send()
    parts.pack_tokens()
    parts.receive()


def exchange(caps, nbins, lengths, visible, dec_grad, tokens, cid):
    return pl.pallas_call(
        functools.partial(exchange_kernel, caps, nbins),
        out_shape=part_outs(caps, nbins),
        in_specs=[vmem(), vmem(), hbm(), hbm()],
        out_specs=(vmem(),) * 8,
        scratch_shapes=part_scratch(caps, nbins),
        compiler_params=pltpu.CompilerParams(collective_id=cid, has_side_effects=True, vmem_limit_bytes=VMEM_LIMIT),
        name="exchange_gradients",
    )(lengths, visible, dec_grad, tokens)


def gather_kernel(
    caps, nbins, dg_hbm, tok_hbm, *refs,
):
    me = Place()
    given, refs = refs[:12], refs[12:]
    w_out, wdn_out, sm_out, part_out, flag_out = refs[:5]
    refs = refs[5:]
    slabs, small, features, s1, r1, s2, r2, s3, r3, given_sem = refs[-22:-12]
    held = refs[-12:]
    len_ref, vis_ref, wq_ref, wo_ref, wu_ref, wd_ref, gain_ref, shift_ref, bias_ref, up_ref, mask_ref, te_ref = held
    loads = [pltpu.make_async_copy(a, b, given_sem.at[n]) for n, (a, b) in enumerate(zip(given, held))]
    for c in loads:
        c.start()
    barrier, count = me.greet()
    parts = Parts(caps, nbins, me, len_ref, vis_ref, dg_hbm, tok_hbm, refs[:8], refs[8:-22])
    parts.load()
    for c in loads:
        c.wait()
    opened, over = parts.prepare()
    half, x2 = me.x // 2, me.x % 2
    lines = (me.y, me.z)
    own = (me.z + half * (me.y - me.z), me.y + half * (me.z - me.y))

    n = MICRO * TRAJ
    group = one_zero((iota((16, n), 1) % TRAJ) // 8 == iota((16, n), 0)).astype(bf16)
    blk = one_zero(iota((SL, SL), 0) // 16 == iota((SL, SL), 1) // 16).astype(bf16)
    pairs = nn_dot(nn_dot(group, opened.astype(bf16)).astype(bf16), blk)
    lane_blk = iota((16, SL), 1) // 16
    room = jnp.zeros((16, SL), f32)
    for j in range(8):
        room = jnp.where(lane_blk == j, float(caps[j]), room)
    crowded = jnp.max(jnp.max(one_zero(pairs > room), axis=1, keepdims=True), axis=0, keepdims=True)
    over = jnp.maximum(over, crowded)

    small[...] = jnp.zeros_like(small)
    small[:, TE : TE + 64] = te_ref[...].astype(f32)
    small[:, BIAS : BIAS + 4] = bias_ref[...].astype(f32)
    small[0:1, UP : UP + 8] = up_ref[...].astype(f32)
    gains, shifts, masks = gain_ref[...].astype(f32), shift_ref[...].astype(f32), mask_ref[...].astype(f32)
    for f in range(2):
        for g in range(2):
            small[f : f + 1, GAIN + g : GAIN + g + 1] = gains[g : g + 1, f : f + 1]
            small[f : f + 1, SHIFT + g : SHIFT + g + 1] = shifts[g : g + 1, f : f + 1]
        small[f : f + 1, MASK : MASK + 1] = masks[:, f : f + 1]
    small[0:1, FLAG : FLAG + 1] = over
    extra = jnp.concatenate([small[...], jnp.zeros((2, SL), f32)], axis=1)
    rows = []
    for f in range(2):
        one = slice(f, f + 1)
        rows += [wq_ref[one, c : c + D].astype(f32) for c in range(0, 3 * D, D)]
        rows += [wo_ref[one, :].astype(f32)]
        rows += [wu_ref[one, c : c + D].astype(f32) for c in range(0, 4 * D, D)]
        rows += [extra[one]]
    slab = jnp.concatenate(rows + [wd_ref[...].astype(f32), jnp.zeros((6, D), f32)], axis=0)
    mine = slabs.at[half, me.core, own[0], own[1], x2]
    mine[...] = slab.astype(bf16)

    pl.semaphore_wait(barrier, count)
    step1 = []
    for d, dx in sorted(((d, dx) for d in range(4) for dx in range(4) if d or dx), key=lambda p: p[0] % 3 + p[1] % 3):
        peer = me.at((me.x + dx) % 4, (me.y + (1 - half) * d) % 4, (me.z + half * d) % 4)
        c = remote(mine, mine, s1.at[4 * d + dx], r1.at[half, own[1], x2], peer)
        c.start()
        step1.append(c)
    for c in parts.loads:
        c.wait()
    sums = parts.send()
    part_out[...] = jnp.zeros_like(part_out)
    part_out[pl.ds(pl.multiple_of(8 * me.seq, 8), 8), :] = sums[:8]
    part_out[MASK : MASK + 1, :] = sums[8:9]
    for h in range(2):
        line = slabs.at[h, me.core, lines[1 - h]]
        for o in range(4):
            for a in range(2):
                @pl.when((me.x != 2 * h + a) | (lines[h] != o))
                def _():
                    arrived(line.at[o, a], r1.at[h, o, a])

    step2, step3 = [], []
    for k in range(3):
        for h in range(2):
            line = slabs.at[h, me.core, lines[1 - h]]
            c = remote(line, line, s2.at[h, k], r2.at[h, k], (me.z_peer, me.y_peer)[h](k + 1))
            c.start()
            step2.append(c)
    for h in range(2):
        line = slabs.at[h, me.core, lines[1 - h]]
        c = remote(line, line, s3.at[h, 0], r3.at[h, 0], me.sibling())
        c.start()
        step3.append(c)
    parts.pack_tokens()
    for k in range(3):
        for h in range(2):
            step2[2 * k + h].wait()
            line = slabs.at[h, me.core, (lines[1 - h] + 3 - k) % 4]
            c = remote(line, line, s3.at[h, k + 1], r3.at[h, k + 1], me.sibling())
            c.start()
            step3.append(c)
    for c in step1:
        c.wait_send()

    pr, pc = iota((D, D), 0), iota((D, D), 1)
    want = jnp.where(
        pr < 144,
        ((pr % 16) // 2) * 32 + (pr % 2) * 9 + pr // 16,
        jnp.where(pr < 208, ((pr - 144) // 8) * 32 + 18 + (pr - 144) % 8, -1),
    )
    perm = one_zero(want == pc).astype(bf16)

    def place(core):
        for x in range(4):
            for z0 in range(2):
                at = 4 * x + 2 * core + z0
                chunk = []
                for z in (2 * z0, 2 * z0 + 1):
                    for y in range(4):
                        a, b = (z, y) if x < 2 else (y, z)
                        chunk.append(slabs[x // 2, core, a, b, x % 2])
                got = nn_dot(perm, jnp.concatenate(chunk, axis=0)).astype(bf16)
                r16 = pl.ds(pl.multiple_of(at * 16, 16), 16)
                for b in range(8):
                    w_out[r16, b * D : (b + 1) * D] = got[16 * b : 16 * b + 16]
                features[r16, :] = got[128:144, :SL]
                wdn_out[pl.ds(pl.multiple_of(at * 64, 64), 64), :] = got[144:208]

    place(me.core)
    parts.receive()
    for c in step3:
        c.wait()
    place(1 - me.core)
    eye = one_zero(iota((SL, SL), 0) == iota((SL, SL), 1)).astype(bf16)
    sm = nt_dot(eye, features[...])
    sm_out[...] = sm
    flag_out[0, 0] = jnp.max(sm[FLAG : FLAG + 1, :]).astype(i32)
    even = one_zero(iota((SL, D), 1) == 2 * iota((SL, D), 0)).astype(bf16)
    by_device = nn_dot(even, features[...]).astype(bf16)
    spread = one_zero(iota((SL, FF), 0) == UP + iota((SL, FF), 1) % 8).astype(bf16)
    wide = jnp.where(iota((SL, FF), 0) == iota((SL, FF), 1) // 8, nn_dot(by_device, spread), 0.0).astype(bf16)
    up = nn_dot(jnp.ones((16, SL), bf16), wide)[:1]
    for c in range(4):
        sm_out[UP + c : UP + c + 1, :] = up[:, c * D : (c + 1) * D]


def gather(caps, nbins, lengths, visible, dec_grad, tokens, shards, cid):
    dma = pltpu.SemaphoreType.DMA
    s = jax.ShapeDtypeStruct
    return pl.pallas_call(
        functools.partial(gather_kernel, caps, nbins),
        out_shape=(
            s((D, 8 * D), bf16), s((FF, D), bf16), s((SL, D), f32), s((SL, D), f32), s((1, 1), i32),
        ) + part_outs(caps, nbins),
        in_specs=[hbm()] * 14,
        out_specs=(vmem(),) * 4 + (smem(),) + (vmem(),) * 8,
        scratch_shapes=part_scratch(caps, nbins) + [
            pltpu.VMEM((2, 2, 4, 4, 2, 32, D), bf16), pltpu.VMEM((2, SL), f32), pltpu.VMEM((D, SL), bf16),
            dma((16,)), dma((2, 4, 2)), dma((2, 3)), dma((2, 3)), dma((2, 4)), dma((2, 4)), dma((12,)),
        ] + [pltpu.VMEM(a.shape, a.dtype) for a in (lengths, visible) + shards],
        compiler_params=pltpu.CompilerParams(collective_id=cid, has_side_effects=True, vmem_limit_bytes=VMEM_MOST),
        name="gather_and_exchange",
    )(dec_grad, tokens, lengths, visible, *shards)


def encoder_kernel(
    nbins, cnt_ref, x_ref, ge_ref, seg_ref, w_ref, wd_ref, sm_ref, part_ref,
    enc_ref, gt_ref, gs_ref,
    gw_scr, gwd_scr, sums_scr, bup_scr, qkv_scr, gqkv_scr,
):
    nsup = (cnt_ref[0, 0] + 1) // 2
    M = 2 * SL
    gw_scr[...] = jnp.zeros_like(gw_scr)
    gwd_scr[...] = jnp.zeros_like(gwd_scr)
    sums_scr[...] = jnp.zeros_like(sums_scr)
    bup_scr[...] = jnp.zeros_like(bup_scr)

    def clear(s, _):
        enc_ref[pl.ds(pl.multiple_of(s * M, M), M), :] = jnp.zeros((M, D), bf16)
        return 0

    lax.fori_loop(nsup, nbins // 2, clear, 0)

    gain1, gain2 = sm_ref[GAIN : GAIN + 1, :], sm_ref[GAIN + 1 : GAIN + 2, :]
    shift1, shift2 = sm_ref[SHIFT : SHIFT + 1, :], sm_ref[SHIFT + 1 : SHIFT + 2, :]
    bq, bv, bo, bd = (sm_ref[BIAS + k : BIAS + 1 + k, :] for k in range(4))
    seg_lo, seg_hi = seg_ref[0:1, :], seg_ref[1:2, :]
    row = iota((SL, SL), 0).astype(f32)
    head0 = iota((SL, SL), 1) < 64
    zero_b = jnp.zeros((SL, SL), bf16)
    ind2 = jnp.concatenate([one_zero(head0), one_zero(~head0)], axis=0).astype(bf16)
    units = [(h, p) for h in range(2) for p in range(2)]

    def two(a):
        return jnp.concatenate([jnp.where(head0, a, zero_b), jnp.where(head0, zero_b, a)], axis=0)

    def body(s, _):
        here = pl.ds(pl.multiple_of(s * M, M), M)
        x = x_ref[here, :].astype(f32)
        cen = x - jnp.mean(x, axis=1, keepdims=True)
        r1 = lax.rsqrt(jnp.mean(cen * cen, axis=1, keepdims=True) + EPS)
        xh1 = cen * r1
        nf = (xh1 * gain1 + shift1).astype(bf16)
        qkv_scr[:, :D] = (nn_dot(nf, w_ref[:, :D]) + bq).astype(bf16) * jnp.asarray(0.125, bf16)
        qkv_scr[:, D : 2 * D] = nn_dot(nf, w_ref[:, D : 2 * D]).astype(bf16)
        qkv_scr[:, 2 * D : 3 * D] = (nn_dot(nf, w_ref[:, 2 * D : 3 * D]) + bv).astype(bf16)

        def unit(h, p):
            rows = slice(h * SL, (h + 1) * SL)
            return [qkv_scr[rows, k * D + p * SL : k * D + (p + 1) * SL] for k in range(3)]

        segs = []
        for h in range(2):
            at = row + ((2 * s + h) * SL).astype(f32)
            seg = one_zero((at >= seg_lo) & (at < seg_hi))
            out = ((seg - 1.0) * BIG).astype(bf16)
            segs.append((seg.astype(bf16), jnp.concatenate([out, out], axis=0)))
        saved = {}
        for h in range(2):
            qkv = [unit(h, p) for p in range(2)]
            sc = [
                nt_dot(
                    jnp.concatenate([qkv[p][0], segs[h][0]], axis=1),
                    jnp.concatenate([two(qkv[p][1]), segs[h][1]], axis=1),
                )
                for p in range(2)
            ]
            top = [[jnp.max(sc[p][:, g * SL : (g + 1) * SL], axis=1, keepdims=True) for g in range(2)] for p in range(2)]
            e = [
                jnp.concatenate(
                    [jnp.exp(sc[p][:, g * SL : (g + 1) * SL] - top[p][g]) for g in range(2)], axis=1
                ).astype(bf16)
                for p in range(2)
            ]
            y = [nn_dot(e[p], jnp.concatenate([two(qkv[p][2]), ind2], axis=1)) for p in range(2)]
            for p in range(2):
                rinv = 1.0 / y[p][:, SL:]
                saved[h, p] = (e[p], rinv, y[p][:, :SL] * rinv)
        att = jnp.concatenate(
            [jnp.concatenate([saved[h, p][2] for p in range(2)], axis=1) for h in range(2)], axis=0
        ).astype(bf16)
        mixed = x + nn_dot(att, w_ref[:, 3 * D : 4 * D]) + bo
        cen = mixed - jnp.mean(mixed, axis=1, keepdims=True)
        r2 = lax.rsqrt(jnp.mean(cen * cen, axis=1, keepdims=True) + EPS)
        xh2 = cen * r2
        ns = (xh2 * gain2 + shift2).astype(bf16)
        ns_t = ns.T
        ge_b = ge_ref[here, :]
        ge_t = ge_b.T
        ge = ge_b.astype(f32)

        enc = mixed + bd
        gns = jnp.zeros((M, D), f32)
        for c in range(4):
            cs = slice(c * D, (c + 1) * D)
            ws = slice(4 * D + c * D, 5 * D + c * D)
            v = nn_dot(ns, w_ref[:, ws]) + sm_ref[UP + c : UP + c + 1, :]
            vv = v * v
            a = 0.5 * jnp.tanh(v * (vv * (GELU_A * GELU_B) + GELU_A)) + 0.5
            hact = v * a
            dg = a + hact * (1.0 - a) * (vv * (6.0 * GELU_A * GELU_B) + 2.0 * GELU_A)
            hb = hact.astype(bf16)
            enc = enc + nn_dot(hb, wd_ref[cs, :])
            ghb = (nt_dot(ge_b, wd_ref[cs, :]) * dg).astype(bf16)
            bup_scr[:, cs] += fold8(ghb.astype(f32))
            gns = gns + nt_dot(ghb, w_ref[:, ws])
            gw_scr[:, ws] += nn_dot(ns_t, ghb)
            gwd_scr[:, cs] += nn_dot(ge_t, hb)
        enc_ref[here, :] = enc.astype(bf16)

        sums_scr[7] += fold8(ge)
        sums_scr[1] += fold8(gns * xh2)
        sums_scr[3] += fold8(gns)
        eg = gns * gain2
        gmix = ge + r2 * (eg - jnp.mean(eg, axis=1, keepdims=True) - xh2 * jnp.mean(eg * xh2, axis=1, keepdims=True))
        gao = gmix.astype(bf16)
        sums_scr[6] += fold8(gao.astype(f32))
        gw_scr[:, 3 * D : 4 * D] += tn_dot(att, gao)
        gatt = nt_dot(gao, w_ref[:, 3 * D : 4 * D])
        for h in range(2):
            rows = slice(h * SL, (h + 1) * SL)
            qkv = [unit(h, p) for p in range(2)]
            da = [gatt[rows, p * SL : (p + 1) * SL] * saved[h, p][1] for p in range(2)]
            dao = [(da[p] * saved[h, p][2]).astype(bf16) for p in range(2)]
            da = [da[p].astype(bf16) for p in range(2)]
            dp = [
                nt_dot(jnp.concatenate([da[p], dao[p]], axis=1), jnp.concatenate([two(qkv[p][2]), -ind2], axis=1))
                for p in range(2)
            ]
            e = [saved[h, p][0] for p in range(2)]
            gsc = [(e[p].astype(f32) * dp[p]).astype(bf16) for p in range(2)]
            gq = [nn_dot(gsc[p], two(qkv[p][1])) * 0.125 for p in range(2)]
            gk = [tn_dot(gsc[p], qkv[p][0]) for p in range(2)]
            gv = [tn_dot(e[p], da[p]) for p in range(2)]
            for p in range(2):
                lanes = slice(p * SL, (p + 1) * SL)
                gqkv_scr[rows, p * SL : (p + 1) * SL] = gq[p].astype(bf16)
                gqkv_scr[rows, D + p * SL : D + (p + 1) * SL] = jnp.where(head0, gk[p][:SL], gk[p][SL:]).astype(bf16)
                gqkv_scr[rows, 2 * D + p * SL : 2 * D + (p + 1) * SL] = jnp.where(head0, gv[p][:SL], gv[p][SL:]).astype(bf16)
        gqkv = gqkv_scr[...]
        sums_scr[4] += fold8(gqkv[:, :D].astype(f32))
        sums_scr[5] += fold8(gqkv[:, 2 * D :].astype(f32))
        gw_scr[:, : 3 * D] += tn_dot(nf, gqkv)
        gnf = nt_dot(gqkv, w_ref[:, : 3 * D])
        sums_scr[0] += fold8(gnf * xh1)
        sums_scr[2] += fold8(gnf)
        eg = gnf * gain1
        gtok = gmix + r1 * (eg - jnp.mean(eg, axis=1, keepdims=True) - xh1 * jnp.mean(eg * xh1, axis=1, keepdims=True))
        hi = gtok.astype(bf16)
        lo = (gtok - hi.astype(f32)).astype(bf16)
        for h in range(2):
            rows = slice(h * SL, (h + 1) * SL)
            gt_ref[2 * s + h, :SL, :] = hi[rows]
            gt_ref[2 * s + h, SL:, :] = lo[rows]
        return 0

    lax.fori_loop(0, nsup, body, 0)

    fin = [jnp.sum(sums_scr[k], axis=0, keepdims=True) for k in range(8)]
    gsm = jnp.concatenate(
        [part_ref[:GAIN, :]] + fin + [part_ref[MASK : MASK + 1, :], jnp.zeros((SL - MASK - 1, D), f32)], axis=0
    ).astype(bf16)
    eye = one_zero(iota((D, D), 0) == iota((D, D), 1)).astype(bf16)
    smt = nt_dot(eye, gsm)
    bup = jnp.sum(bup_scr[...], axis=0, keepdims=True).astype(bf16)
    dsel = iota((SL, FF), 0) == iota((SL, FF), 1) // 8
    bup_m = jnp.where(dsel, jnp.broadcast_to(bup, (SL, FF)), jnp.zeros((SL, FF), bf16))
    rep = one_zero(iota((SL, FF), 0) == UP + iota((SL, FF), 1) % 8).astype(bf16)
    bup_d = nt_dot(bup_m, rep)
    even = one_zero(iota((D, SL), 0) == 2 * iota((D, SL), 1)).astype(bf16)
    smt = (smt + nn_dot(even, bup_d.astype(bf16))).astype(bf16)
    gwd_t = [nt_dot(eye, gwd_scr[:, c * D : (c + 1) * D].astype(bf16)).astype(bf16) for c in range(4)]
    pr, pc = iota((D, D), 0), iota((D, D), 1)
    pd, prr = pr // 32, pr % 32
    want = jnp.where(prr < 18, (prr % 9) * 16 + pd * 2 + prr // 9, jnp.where(prr < 26, 144 + pd * 8 + prr - 18, -1))
    perm = one_zero(want == pc).astype(bf16)
    sm_pad = jnp.zeros((16, SL), bf16)
    tail = jnp.zeros((48, D), bf16)
    for qn in range(16):
        r16 = slice(qn * 16, qn * 16 + 16)
        parts = [gw_scr[r16, bb * D : (bb + 1) * D].astype(bf16) for bb in range(8)]
        parts.append(jnp.concatenate([smt[r16], sm_pad], axis=1))
        o = (qn % 4) * 64
        parts.append(gwd_t[qn // 4][o : o + 64])
        parts.append(tail)
        gs_ref[qn] = nn_dot(perm, jnp.concatenate(parts, axis=0)).astype(bf16)


def encoder(nbins, cnt, x, ge, seg, w, wd, sm, part):
    return pl.pallas_call(
        functools.partial(encoder_kernel, nbins),
        out_shape=(
            jax.ShapeDtypeStruct((nbins * SL, D), bf16),
            jax.ShapeDtypeStruct((nbins, 2 * SL, D), bf16),
            jax.ShapeDtypeStruct((16, D, D), bf16),
        ),
        in_specs=[pl.BlockSpec(memory_space=pltpu.SMEM)] + [vmem()] * 7,
        out_specs=(vmem(),) * 3,
        scratch_shapes=[
            pltpu.VMEM((D, 2048), f32), pltpu.VMEM((D, FF), f32), pltpu.VMEM((8, 8, D), f32), pltpu.VMEM((8, FF), f32),
            pltpu.VMEM((2 * SL, 3 * D), bf16), pltpu.VMEM((2 * SL, 3 * D), bf16),
        ],
        compiler_params=pltpu.CompilerParams(vmem_limit_bytes=VMEM_LIMIT),
        name="encoder_fwd_bwd",
    )(cnt, x, ge, seg, w, wd, sm, part)


def pack_encoded(caps, nbins, enc_ref, src_ref, s_scr):
    total = sum(caps)
    row = iota((256, SL), 0).astype(f32)
    for c in range(0, total, 256):
        wide = min(256, total - c)

        def one(b, acc):
            src = src_ref[pl.ds(pl.multiple_of(b * 16, 16), 16), :]
            hit = [one_zero(row[:wide] + float(c + 1) == src[8 * k : 8 * k + 1]) for k in range(2)]
            rows = enc_ref[pl.ds(pl.multiple_of(b * 256, 256), 256), :]
            return acc + nn_dot(jnp.concatenate(hit, axis=1).astype(bf16), rows)

        s_scr[c : c + wide, :] = lax.fori_loop(0, nbins // 2, one, jnp.zeros((wide, D), f32)).astype(bf16)


def scatter_kernel(
    caps, nbins, bins_ref, gs_ref, enc_ref, src_ref, gt_ref, slot_ref, cols_ref, sm_ref,
    dec_out, gtok_out, slab_out,
    got1, sum1, got2, sum2, got3, s_scr, rows_scr, s_sem, r_sem, s1, r1, s2, r2, s3, r3, own_sem,
):
    me = Place()
    base = bases(caps)
    most, room = decode_room(caps)
    steps = sm_ref[pl.ds(pl.multiple_of(TE + 8 * me.seq, 8), 8), :]
    extra = jnp.concatenate([sm_ref[MASK : MASK + 1, :], steps, jnp.zeros((room - most - 9, D), f32)], axis=0).astype(bf16)
    for i in range(8):
        rows_scr[i, :most] = jnp.zeros((most, D), bf16)
        rows_scr[i, most:] = extra
    barrier, count = me.greet()
    pl.semaphore_wait(barrier, count)

    step1 = []
    for x in (0, 2, 1, 3):
        c = remote(gs_ref.at[x, 1 - me.core], got1.at[x], s1.at[x], r1.at[x], me.sibling())
        c.start()
        step1.append((x, c))
    pack_encoded(caps, nbins, enc_ref, src_ref, s_scr)
    for j in range(8):
        part = s_scr.at[pl.ds(base[j], caps[j])]
        there = rows_scr.at[me.seq, pl.ds(0, caps[j])]

        @pl.when(me.seq == j)
        def _():
            pltpu.make_async_copy(part, there, own_sem).start()

        @pl.when(me.seq != j)
        def _():
            remote(part, there, s_sem.at[j], r_sem.at[me.seq], (j, me.dp)).start()

    def unpack(first, last):
        lane = iota((SL, SL), 1).astype(f32)
        for t in range(first, last):
            hit = one_zero(slot_ref[:, t : t + 1] == lane).astype(bf16)
            gtok_out[t] = nn_dot(jnp.concatenate([hit, hit], axis=1), gt_ref[bins_ref[0, t]])

    unpack(0, 8)
    for x, c in step1:
        c.wait()
        for z in range(4):
            for y in range(4):
                total = gs_ref[x, me.core, 4 * z + y].astype(f32) + got1[x, 4 * z + y].astype(f32)
                if x < 2:
                    sum1[0, z, x % 2, y] = total.astype(bf16)
                else:
                    sum1[1, y, x % 2, z] = total.astype(bf16)
    first = (me.z, me.y)
    second = (me.y, me.z)
    peers = (me.z_peer, me.y_peer)
    step2 = []
    for k in (2, 1, 3):
        for h in range(2):
            c = remote(sum1.at[h, (first[h] + k) % 4], got2.at[h, k - 1], s2.at[h, k - 1], r2.at[h, k - 1], peers[h](k))
            c.start()
            step2.append(c)
    unpack(8, NT)
    for c in step2:
        c.wait()
    for h in range(2):
        for x2 in range(2):
            for o in range(4):
                total = sum1[h, first[h], x2, o].astype(f32)
                for k in range(3):
                    total = total + got2[h, k, x2, o].astype(f32)
                sum2[h, x2, o] = total.astype(bf16)

    half = me.x // 2
    mine = second[0] + half * (second[1] - second[0])
    for h in range(2):
        for x2 in range(2):
            for o in range(4):
                is_me = (me.x == 2 * h + x2) & (second[h] == o)
                peer = me.at(2 * h + x2, o if h == 0 else me.y, me.z if h == 0 else o)

                @pl.when(is_me)
                def _():
                    got3[o, 2 * h + x2] = sum2[h, x2, o]

                @pl.when(jnp.logical_not(is_me))
                def _():
                    remote(
                        sum2.at[h, x2, o], got3.at[second[h], me.x], s3.at[h, x2, o], r3.at[second[h], me.x], peer
                    ).start()

    lane = iota((PART, SL), 1).astype(f32)
    cols = cols_ref[...]
    for j in range(8):
        @pl.when(me.seq == j)
        def _():
            here = rows_scr.at[0, pl.ds(0, caps[j])]
            for i in range(8):
                if i != j:
                    arrived(here, r_sem.at[i])
            arrived(here, own_sem)

        @pl.when(me.seq != j)
        def _():
            arrived(s_scr.at[pl.ds(base[j], caps[j])], s_sem.at[j])
    for i in range(8):
        hit = []
        for c in range(0, room, SL):
            one = cols[:, i : i + 1] == lane + float(c)
            if c + SL > most:
                one = one | (cols[:, 8 + i : 9 + i] == lane + float(c))
            hit.append(one_zero(one))
        got = nn_dot(jnp.concatenate(hit, axis=1).astype(bf16), rows_scr[i]).astype(bf16)
        dec_out[:, 8 * i : 8 * i + 8] = got.reshape(MICRO, 8, 16, D)

    for o in range(4):
        for x in range(4):
            is_me = (me.x == x) & (mine == o)

            @pl.when(jnp.logical_not(is_me))
            def _():
                arrived(got3.at[o, x], r3.at[o, x])
    for h in range(2):
        for x2 in range(2):
            for o in range(4):
                is_me = (me.x == 2 * h + x2) & (second[h] == o)

                @pl.when(jnp.logical_not(is_me))
                def _():
                    arrived(sum2.at[h, x2, o], s3.at[h, x2, o])
    slab = jnp.zeros((32, D), f32)
    for o in range(4):
        for x in range(4):
            slab = slab + got3[o, x].astype(f32)

    slab_out[...] = slab


def scatter(caps, nbins, bins, gs, enc, src, gt, slot, cols, sm, cid):
    dma = pltpu.SemaphoreType.DMA
    most, room = decode_room(caps)
    s = jax.ShapeDtypeStruct
    return pl.pallas_call(
        functools.partial(scatter_kernel, caps, nbins),
        out_shape=(
            s((MICRO, TRAJ, 16, D), bf16), s((NT, SL, D), f32), s((32, D), f32),
        ),
        in_specs=[smem()] + [vmem()] * 7,
        out_specs=(vmem(),) * 3,
        scratch_shapes=[
            pltpu.VMEM((4, 16, 32, D), bf16), pltpu.VMEM((2, 4, 2, 4, 32, D), bf16),
            pltpu.VMEM((2, 3, 2, 4, 32, D), bf16), pltpu.VMEM((2, 2, 4, 32, D), bf16),
            pltpu.VMEM((4, 4, 32, D), bf16), pltpu.VMEM((sum(caps), D), bf16), pltpu.VMEM((8, room, D), bf16),
            dma((8,)), dma((8,)), dma((4,)), dma((4,)), dma((2, 3)), dma((2, 3)), dma((2, 2, 4)), dma((4, 4)), dma,
        ],
        compiler_params=pltpu.CompilerParams(collective_id=cid, has_side_effects=True, vmem_limit_bytes=VMEM_LIMIT),
        name="scatter_and_exchange",
    )(bins, gs, enc, src, gt, slot, cols, sm)


def finish_kernel(
    dec_ref, gtok_ref, slab_ref,
    dec_out, gtok_out, gain_out, shift_out, wq_out, wo_out, wu_out, wd_out, bias_out, up_out, mask_out, te_out, sems,
):
    copies = [
        pltpu.make_async_copy(dec_ref, dec_out, sems.at[0]), pltpu.make_async_copy(gtok_ref, gtok_out, sems.at[1])
    ]
    for c in copies:
        c.start()
    slab = slab_ref[...]
    for f in range(2):
        one = slice(f, f + 1)
        for b in range(3):
            wq_out[one, b * D : (b + 1) * D] = slab[9 * f + b : 9 * f + b + 1]
        wo_out[one, :] = slab[9 * f + 3 : 9 * f + 4]
        for b in range(4):
            wu_out[one, b * D : (b + 1) * D] = slab[9 * f + 4 + b : 9 * f + 5 + b]
        row = slab[9 * f + 8 : 9 * f + 9]
        te_out[one, :] = row[:, TE : TE + 64]
        bias_out[one, :] = row[:, BIAS : BIAS + 4]
        mask_out[:, one] = row[:, MASK : MASK + 1]
        for g in range(2):
            gain_out[g : g + 1, one] = row[:, GAIN + g : GAIN + g + 1]
            shift_out[g : g + 1, one] = row[:, SHIFT + g : SHIFT + g + 1]
    wd_out[...] = slab[18:26]
    up_out[...] = slab[8:9, UP : UP + 8]
    for c in copies:
        c.wait()


def finish(dec, gtok, slab):
    s = jax.ShapeDtypeStruct
    return pl.pallas_call(
        finish_kernel,
        out_shape=(
            s(dec.shape, dec.dtype), s(gtok.shape, gtok.dtype), s((2, 2), f32), s((2, 2), f32), s((2, 3 * D), f32),
            s((2, D), f32), s((2, FF), f32), s((8, D), f32), s((2, 4), f32), s((1, 8), f32), s((1, 2), f32),
            s((2, 64), f32),
        ),
        in_specs=[vmem()] * 3,
        out_specs=(hbm(),) * 2 + (vmem(),) * 10,
        scratch_shapes=[pltpu.SemaphoreType.DMA((2,))],
        compiler_params=pltpu.CompilerParams(vmem_limit_bytes=VMEM_LIMIT),
        name="results",
    )(dec, gtok, slab)


def per_device(
    tokens, lengths, visible, norm_gains, norm_biases, w_qkv, w_out, w_up, w_down, proj_biases, up_bias, mask_token,
    time_embed, dec_grad,
):
    lengths, visible = lengths[:, 0], visible[:, 0]
    tok = tokens.reshape(NT, SL, D)
    dg = dec_grad[:, 0]
    shards = (
        w_qkv, w_out, w_up, w_down, norm_gains, norm_biases, proj_biases.T, up_bias[None], mask_token[None], time_embed.T
    )
    w, wd, sm, part, flag, *packed = gather(CAPS, NBINS, lengths, visible, dg, tok, shards, 0)

    def rest(caps, nbins, packed, cid):
        x, ge, seg, src, slot, bins, count, cols = packed
        enc, gt, gs = encoder(nbins, count, x, ge, seg, w, wd, sm, part)
        out = scatter(caps, nbins, bins, gs.reshape(4, 2, 16, 32, D), enc, src, gt, slot, cols, sm, cid)
        return tuple(finish(*out))

    def roomy():
        return rest(FULL, NFULL, exchange(FULL, NFULL, lengths, visible, dg, tok, 1), 2)

    outs = lax.cond(flag[0, 0] > 0, roomy, lambda: rest(CAPS, NBINS, packed, 3))
    dec, gtok, gain, shift, wq, wo, wu, wdn, bias, up, mask, te = outs
    return (
        dec.reshape(MICRO, 1, TRAJ, 16, D), gtok.reshape(MICRO, 1, 8, SL, D), gain, shift, wq, wo, wu, wdn, bias.T,
        up.reshape(8), mask.reshape(2), te.T,
    )


def solution(mesh):
    everyone = ("seq", "dp")
    return jax.shard_map(
        per_device,
        mesh=mesh,
        in_specs=(
            P(None, "dp", "seq", None, None), P(None, "dp", None), P(None, "dp", None, None), P(None, everyone),
            P(None, everyone), P(everyone, None), P(everyone, None), P(everyone, None), P(everyone, None),
            P(None, everyone), P(everyone), P(everyone), P(None, everyone), P(None, "dp", None, "seq", None),
        ),
        out_specs=(
            P(None, "dp", None, "seq", None), P(None, "dp", "seq", None, None), P(None, everyone), P(None, everyone),
            P(everyone, None), P(everyone, None), P(everyone, None), P(everyone, None), P(None, everyone), P(everyone),
            P(everyone), P(None, everyone),
        ),
        check_vma=False,
    )
```
